32 devices in a mesh: cell: 32 (over z, y, x, core).
Axes of the slice: x: 2, y: 2, z: 4, core: 2. Of those that a mesh axis runs over, the one named last changes fastest.
Arguments:
- splats: float32 [9, 65536], P(None, 'cell'), may hold values from -6 to 20, as said below
- target: float32 [3, 131072], P(None, 'cell'), may hold values from 0 to 1
- slot_owner: int32 [512, 256, 1], P('cell'), may hold values from 0 to 31; in each aligned block of 4096 rows (0 to 4095, 4096 to 8191, ..., all dimensions but the last counted through in order) at most 256 rows name the same one
- slot_row: int32 [512, 256], P('cell'), may hold values from 0 to 2047
- depth_order: int32 [512, 256], P('cell'), may hold values from 0 to 255, each once within a row
- tile_count: int32 [512], P('cell'), may hold values from 64 to 256
Outputs:
- rendered: float32 [3, 131072], P(None, 'cell')
- grad_splats: float32 [9, 65536], P(None, 'cell')
The draws below stay inside these ranges and needn't reach their ends.
Inputs may be any that keep to these rules, and one draw needn't show every extreme that they name: Rows of splats: mean x and y in tile pixels, entries a, b, c of the factor of the inverse covariance (a and c positive), opacity logit, red, green, blue. `slot_owner`: among the slots of one device's 16 tiles no cell is named more than 256 times; in some devices' tiles some cell is named exactly 256 times.
All inputs are finite; a program needn't handle non-finite values.
Results may differ from the reference program's by a relative error of at most 0.00021.
Values sent between devices are 32-bit elements; how exact they have to be, the bound alone decides.
A program may use at most 320 MiB of HBM per device.

```python
import math
import jax
import jax.numpy as jnp
import numpy as np
from jax import lax

G_DEV = 2048
T_DEV = 16
BLOCK = 256
SIDE = 16
TILES = 512
G = 65536
PIXELS = 131072
CAP = 256
N_CELL = 32


def draw_splats(key, part):
    key = jax.random.fold_in(key, 11)
    keys = jax.random.split(key, 5)
    means = jnp.clip(0.5 * SIDE + 0.3 * SIDE * jax.random.normal(keys[0], (2, G), jnp.float32), -0.25 * SIDE, 1.25 * SIDE)
    factors = jnp.exp(jax.random.uniform(keys[1], (2, G), jnp.float32, jnp.log(2.0 / SIDE), jnp.log(8.0 / SIDE)))
    colours = jax.random.uniform(keys[4], (3, G), jnp.float32)
    shear = jax.random.uniform(keys[2], (1, G), jnp.float32, -2.0 / SIDE, 2.0 / SIDE)
    logits = jax.random.uniform(keys[3], (1, G), jnp.float32, -6.0, -2.0)
    return jnp.concatenate([means, factors[0:1], shear, factors[1:2], logits, colours], axis=0)


def place_ends(result, own_key, smallest, largest):
    dims = result.shape
    place = [jax.random.randint(jax.random.fold_in(own_key, axis), (), 0, dims[axis]) for axis in range(len(dims))]
    result = result.at[tuple(place)].set(smallest)
    longest = dims.index(max(dims))
    place[longest] = (place[longest] + 1) % dims[longest]
    return result.at[tuple(place)].set(largest)


def block_scale(stream_key, extent, pieces, low, top_value):
    def one(axis_at, parts):
        heights = jax.random.uniform(jax.random.fold_in(jax.random.fold_in(stream_key, 6), axis_at), (parts,), jnp.float32, low / len(pieces), top_value / len(pieces))
        return jnp.repeat(jnp.exp(heights), extent[axis_at] // parts).reshape((-1,) + (1,) * (len(extent) - axis_at - 1))

    factor_of = one(*pieces[0])
    for cut in pieces[1:]:
        factor_of = factor_of * one(*cut)
    return factor_of


def shared_out(own_key, own, number, rows, amount, top, reach, slope):
    ranking = jax.random.permutation(own_key, amount)
    crowded, common = shares(amount, rows * top, reach, slope, True), shares(amount, rows * top, reach, slope, False)
    places = jnp.arange(amount)

    def named(lengths, offset_by):
        used = int((lengths > 0).sum())
        fixed = max(1, used // 4)
        passed = fixed + (places - fixed + offset_by * (used - fixed)) % max(1, amount - fixed)
        return jnp.zeros((amount,), jnp.int32).at[ranking[jnp.where(places < fixed, places, passed)]].set(jnp.asarray(lengths, jnp.int32))

    lengths = jnp.where(number % 4 == 0, named(crowded, number // 4), named(common, number - number // 4 - 1))
    mixed = jax.random.permutation(jax.random.fold_in(own, 3), amount)
    donor, receiver = mixed[0:amount // 2 * 2:2], mixed[1:amount // 2 * 2:2]
    margin = jnp.minimum(lengths[donor] - 1, reach - lengths[receiver]) // 2
    margin = jnp.where((donor == ranking[0]) | (receiver == ranking[0]) | (lengths[receiver] == 0), 0, jnp.maximum(margin, 0))
    passed = jax.random.randint(jax.random.fold_in(own, 4), (amount // 2,), 0, 1 << 20) % (margin + 1)
    lengths = lengths.at[donor].add(-passed).at[receiver].add(passed)
    members = jnp.searchsorted(jnp.cumsum(lengths), jnp.arange(rows * top), side="right").astype(jnp.int32)
    grid = members.reshape(top, rows).T
    grid = grid[jax.random.permutation(jax.random.fold_in(own, 1), rows)]
    offset_by = jax.random.randint(jax.random.fold_in(own, 2), (rows, 1), 0, top)
    return jnp.take_along_axis(grid, (jnp.arange(top)[None, :] + offset_by) % top, axis=1)


def shares(number_of, total, most, slope, full):
    loads = [(1 << 20) // math.isqrt(standing ** slope) + 1 for standing in range(1, number_of + 1)]
    largest = most if full else min(most, max(-(-total // number_of), total * loads[0] // sum(loads)))
    least = 1 if total - largest >= number_of - 1 else 0
    given, rest = [largest] + [least] * (number_of - 1), total - largest - least * (number_of - 1)
    while rest > 0:
        candidates = [i for i in range(1, number_of) if given[i] < largest] or [i for i in range(1, number_of) if given[i] < most]
        whole, left = sum([loads[i] for i in candidates]), rest
        for i in candidates:
            addition = min(most - given[i], max(1, left * loads[i] // whole), rest)
            given[i] = given[i] + addition
            rest = rest - addition
    return np.array(given)


def setup_inputs(seed: int = 0) -> dict:
    seeds = jax.random.split(jax.random.key(seed), 7)
    splats = draw_splats(jax.random.fold_in(seeds[6], 71), 0)
    target = jnp.clip(1.0 * jax.random.uniform(seeds[1], (3, PIXELS), jnp.float32) ** block_scale(seeds[1], (3, PIXELS), ((1, 32),), -0.2, 0.2), 0.0, 1.0)
    slot_owner_keys = jax.random.split(jax.random.fold_in(seeds[2], 1), TILES * BLOCK // (T_DEV * BLOCK))
    slot_owner_turns = jax.random.permutation(jax.random.fold_in(seeds[2], 3), TILES * BLOCK // (T_DEV * BLOCK))
    slot_owner = jax.vmap(lambda own, number: shared_out(jax.random.fold_in(seeds[2], 2), own, number, T_DEV * BLOCK, N_CELL, 1, CAP, 2))(slot_owner_keys, slot_owner_turns).reshape((TILES, BLOCK, 1))
    slot_row = place_ends(jax.random.randint(seeds[3], (TILES, BLOCK), 0, G_DEV), jax.random.fold_in(seeds[3], 1), 0, G_DEV - 1).astype(jnp.int32)
    depth_order = jax.vmap(lambda own: jax.random.permutation(own, BLOCK))(jax.random.split(seeds[4], TILES)).reshape((TILES, BLOCK)).astype(jnp.int32)
    tile_count = place_ends(jax.random.randint(seeds[5], (TILES,), BLOCK // 4, BLOCK + 1), jax.random.fold_in(seeds[5], 1), BLOCK // 4, BLOCK).astype(jnp.int32)
    return {"splats": splats, "target": target, "slot_owner": slot_owner, "slot_row": slot_row, "depth_order": depth_order, "tile_count": tile_count}


tile_group = 8

def shade_tile(params, live_mask, target_tile):
    pixel_index = jnp.arange(SIDE * SIDE)
    pixel_x = (pixel_index % SIDE).astype(jnp.float32) + 0.5
    pixel_y = (pixel_index // SIDE).astype(jnp.float32) + 0.5
    diff_x = pixel_x[None, :] - params[0][:, None]
    diff_y = pixel_y[None, :] - params[1][:, None]
    first_axis = params[2][:, None] * diff_x + params[3][:, None] * diff_y
    second_axis = params[4][:, None] * diff_y
    opacity = jax.nn.sigmoid(params[5]) * live_mask
    alpha = opacity[:, None] * jnp.exp(-0.5 * (first_axis * first_axis + second_axis * second_axis))
    survive = 1.0 - alpha
    transmit = jnp.cumprod(survive, axis=0) / survive
    picture = jnp.dot(params[6:9], transmit * alpha, precision=lax.Precision.HIGHEST)
    error_sum = 0.5 * jnp.sum((picture - target_tile) ** 2)
    return (error_sum, picture)

def tile_gradient(params, live_mask, target_tile):
    (error_sum, picture), slot_grads = jax.value_and_grad(shade_tile, has_aux=True)(params, live_mask, target_tile)
    return (picture, slot_grads)

def group_rows(array):
    return array.reshape((array.shape[0] // tile_group, tile_group) + array.shape[1:])

def reference(splats, target, slot_owner, slot_row, depth_order, tile_count):
    tiles = slot_row.shape[0]
    global_ids = slot_owner[:, :, 0] * G_DEV + slot_row
    global_ids = jnp.take_along_axis(global_ids, depth_order, axis=1)
    live_mask = (depth_order < tile_count[:, None]).astype(jnp.float32)
    targets = target.reshape(3, tiles, SIDE * SIDE).transpose(1, 0, 2)

    def per_group(packed):
        group_ids, group_live, group_target = packed
        params = jnp.take(splats, group_ids, axis=1).transpose(1, 0, 2)
        return jax.vmap(tile_gradient)(params, group_live, group_target)
    pictures, grads = lax.map(per_group, (group_rows(global_ids), group_rows(live_mask), group_rows(targets)))
    rendered = pictures.reshape(tiles, 3, -1).transpose(1, 0, 2).reshape(3, -1)
    slot_grads = grads.reshape(tiles, 9, -1).transpose(1, 0, 2).reshape(9, -1)
    grad_splats = jnp.zeros((9, splats.shape[1]), jnp.float32).at[:, global_ids.reshape(-1)].add(slot_grads)
    return (rendered, grad_splats)
```

```python
import functools

import jax
import jax.numpy as jnp
from jax import lax
from jax.experimental import pallas as pl
from jax.experimental.pallas import tpu as pltpu
from jax.sharding import PartitionSpec as P

SIDE = 16
PIX = SIDE * SIDE
ROWS = 16
PARAMS = 9
LANES = 128
F32, BF16, I32 = jnp.float32, jnp.bfloat16, jnp.int32
NT = (((1,), (1,)), ((), ()))
TN = (((0,), (0,)), ((), ()))


def split(x, parts):
    out = []
    for part in range(parts):
        out.append(x.astype(BF16))
        if part < parts - 1:
            x = x - out[-1].astype(F32)
    return out


def dot(a, b, dims=(((1,), (0,)), ((), ()))):
    return lax.dot_general(a, b, dims, preferred_element_type=F32)


def iota(shape, axis):
    return lax.broadcasted_iota(I32, shape, axis)


def one_hot(index, count):
    return jnp.where(iota((count, index.shape[1]), 0) == index, 1.0, 0.0)


def pad_rows(pieces, count):
    have = sum(piece.shape[0] for piece in pieces)
    if have < count:
        pieces = list(pieces) + [jnp.zeros((count - have, pieces[0].shape[1]), F32)]
    return jnp.concatenate(pieces, axis=0)


def plan_slots(order_ref, owner_ref, row_ref, own_ref, pos_ref, ask_ref, parts_ref):
    tiles, block = order_ref.shape
    cells, cap = ask_ref.shape
    before = jnp.where(iota((block, block), 0) < iota((block, block), 1), 1.0, 0.0).astype(BF16)
    parts_ref[...] = jnp.zeros_like(parts_ref)

    def tile(t, seen):
        at = pl.ds(t, 1)
        chosen = one_hot(order_ref[at, :], block).astype(BF16)
        row = row_ref[at, :]
        source = pad_rows(
            [owner_ref[at, :].astype(F32), (row >> 8).astype(F32), (row & 255).astype(F32)], 16
        )
        moved = dot(source.astype(BF16), chosen)
        own = moved[0:1].astype(I32)
        mine = one_hot(own, cells)
        earlier = dot(mine.astype(BF16), before) + seen
        pos = jnp.sum(mine * earlier, axis=0, keepdims=True).astype(I32)
        own_ref[at, :] = own
        pos_ref[at, :] = pos
        asked = jnp.concatenate([mine * moved[1:2], mine * moved[2:3]], axis=0).astype(BF16)
        parts_ref[...] += dot(asked, one_hot(pos, cap).astype(BF16), NT)
        return seen + jnp.sum(mine, axis=1, keepdims=True)

    lax.fori_loop(0, tiles, tile, jnp.zeros((cells, 1), F32))
    both = parts_ref[...].astype(I32)
    ask_ref[...] = both[:cells] * 256 + both[cells:]


def answer(splats_ref, rows_ref, values_ref):
    cells, cap = rows_ref.shape
    groups = splats_ref.shape[1] // LANES
    table = jnp.concatenate(
        [pad_rows([splats_ref[:, g * LANES : (g + 1) * LANES]], ROWS) for g in range(groups)], axis=0
    )
    table = jnp.concatenate(split(table, 3), axis=1)

    def cell(c, carry):
        row = rows_ref[pl.ds(c, 1), :]
        low = one_hot(row & (LANES - 1), LANES).astype(BF16)
        found = dot(table, jnp.concatenate([low, low, low], axis=0))
        high = row // LANES
        total = jnp.zeros((ROWS, cap), F32)
        for g in range(groups):
            total += jnp.where(high == g, found[g * ROWS : (g + 1) * ROWS], 0.0)
        values_ref[pl.ds(c, 1)] = total[None]
        return carry

    lax.fori_loop(0, cells, cell, 0)


def scan_rows(x, keep, fill, down, combine):
    at = iota(x.shape, 0)

    def moved(y, by):
        if down:
            return jnp.where(at >= by, pltpu.roll(y, by, 0), fill)
        return jnp.where(at < 8 - by, pltpu.roll(y, 8 - by, 0), fill)

    x = moved(x, 1)
    for by in (1, 2, 4):
        x = combine(x, moved(x, by))
    return x


def shade(
    values_ref, own_ref, pos_ref, order_ref, count_ref, target_ref, rendered_ref, out_ref,
    table_ref, f1_ref, f2_ref, alpha_ref, w_ref, h_ref,
):
    tiles, block = own_ref.shape
    cells, _, cap = values_ref.shape
    steps = block // 8
    pixel = iota((1, PIX), 1)
    x = (pixel % SIDE).astype(F32) + (0.5 - SIDE / 2)
    y = (pixel // SIDE).astype(F32) + (0.5 - SIDE / 2)
    one, zero = jnp.ones((1, PIX), F32), jnp.zeros((1, PIX), F32)
    linear = jnp.concatenate(
        [
            pad_rows([x, y, one], 8),
            pad_rows([zero, zero, zero, y, one], 8),
            pad_rows([zero, zero, zero, zero, zero, one], 8),
        ],
        axis=1,
    )
    linear = pad_rows([linear, linear, linear], 32).astype(BF16)
    moments = pad_rows([one, x, y], 16).astype(BF16)

    for c in range(cells):
        for part, piece in enumerate(split(values_ref[c], 3)):
            table_ref[c * ROWS : (c + 1) * ROWS, part * cap : (part + 1) * cap] = piece
    out_ref[...] = jnp.zeros_like(out_ref)

    def tile(t, carry):
        at = pl.ds(t, 1)
        own = own_ref[at, :]
        place = one_hot(pos_ref[at, :], cap).astype(BF16)
        found = dot(table_ref[...], jnp.concatenate([place, place, place], axis=0))
        p = jnp.zeros((ROWS, block), F32)
        for c in range(cells):
            p += jnp.where(own == c, found[c * ROWS : (c + 1) * ROWS], 0.0)
        live = jnp.where(order_ref[at, :] < count_ref[at, :], 1.0, 0.0)
        mx, my = p[0:1] - SIDE / 2, p[1:2] - SIDE / 2
        a, b, c2 = p[2:3], p[3:4], p[4:5]
        colour = p[6:9]
        sig = 1.0 / (1.0 + jnp.exp(-p[5:6]))
        unsig = 1.0 / (1.0 + jnp.exp(p[5:6]))
        factors = pad_rows([a, b, -(a * mx + b * my), c2, -(c2 * my), sig * live], 8)
        factors = pad_rows([z.astype(F32) for z in split(factors, 3)], 32).astype(BF16)
        spread = dot(factors, linear, TN)
        f1, f2 = spread[:, :PIX], spread[:, PIX : 2 * PIX]
        f1_ref[...] = f1
        f2_ref[...] = f2
        alpha_ref[...] = spread[:, 2 * PIX :] * jnp.exp(-0.5 * (f1 * f1 + f2 * f2))

        run = jnp.ones((8, PIX), F32)
        for v in range(steps):
            alpha = alpha_ref[8 * v : 8 * v + 8, :]
            w_ref[8 * v : 8 * v + 8, :] = run * alpha
            run = run * (1.0 - alpha)
        ahead = scan_rows(run, None, 1.0, True, lambda u, w: u * w)
        for v in range(steps):
            w_ref[8 * v : 8 * v + 8, :] *= ahead

        colours = [z.astype(F32) for z in split(colour, 3)]
        ch, cm, cl = colours
        wh, wl = split(w_ref[...], 2)
        stacked = pad_rows(colours, 16).astype(BF16)
        picture = dot(stacked, wh) + dot(stacked, wl)
        picture = picture[0:3] + picture[3:6] + picture[6:9]
        lanes = pl.ds(pl.multiple_of(t * PIX, PIX), PIX)
        rendered_ref[:, lanes] = picture
        error = picture - target_ref[:, lanes]
        errors = [z.astype(F32) for z in split(error, 3)]
        eh, em, el = errors
        dw = dot(
            pad_rows([ch, ch, ch, cm, cm, cl], 32).astype(BF16),
            pad_rows([eh, em, el, eh, em, eh], 32).astype(BF16),
            TN,
        )
        stacked = pad_rows(errors, 16).astype(BF16)
        dcol = dot(stacked, wh, NT) + dot(stacked, wl, NT)
        dcol = dcol[0:3] + dcol[3:6] + dcol[6:9]

        h_ref[...] = dw * w_ref[...]
        run = jnp.zeros((8, PIX), F32)
        for v in range(steps):
            run = run + h_ref[8 * v : 8 * v + 8, :]
        behind = scan_rows(run, None, 0.0, False, lambda u, w: u + w)
        for v in reversed(range(steps)):
            alpha = alpha_ref[8 * v : 8 * v + 8, :]
            u = h_ref[8 * v : 8 * v + 8, :]
            h_ref[8 * v : 8 * v + 8, :] = u - behind * (alpha / (1.0 - alpha))
            behind = behind + u

        h = h_ref[...]

        def moment(z):
            zh, zl = split(z, 2)
            return dot(moments, zh, NT) + dot(moments, zl, NT)

        m0, m1, m2 = moment(h), moment(-h * f1_ref[...]), moment(-h * f2_ref[...])
        s1, s2 = m1[0:1], m2[0:1]
        grads = pad_rows(
            [
                -a * s1,
                -b * s1 - c2 * s2,
                m1[1:2] - mx * s1,
                m1[2:3] - my * s1,
                m2[2:3] - my * s2,
                unsig * m0[0:1],
                dcol,
            ],
            ROWS,
        )
        sent = jnp.concatenate([jnp.where(own == c, grads, 0.0) for c in range(cells)], axis=0)
        sent = jnp.concatenate(split(sent, 3), axis=1)
        put = dot(sent, jnp.concatenate([place, place, place], axis=1), NT)
        out_ref[...] += put.reshape(out_ref.shape)
        return carry

    lax.fori_loop(0, tiles, tile, 0)


def collect(incoming_ref, rows_ref, grad_ref, total_ref):
    cells, _, cap = incoming_ref.shape
    groups = grad_ref.shape[1] // LANES
    total_ref[...] = jnp.zeros_like(total_ref)

    def cell(c, carry):
        row = rows_ref[pl.ds(c, 1), :]
        low = one_hot(row & (LANES - 1), LANES).astype(BF16)
        high = row // LANES
        part = incoming_ref[pl.ds(c, 1)][0]
        placed = jnp.concatenate([jnp.where(high == g, part, 0.0) for g in range(groups)], axis=0)
        placed = jnp.concatenate(split(placed, 3), axis=1)
        total_ref[...] += dot(placed, jnp.concatenate([low, low, low], axis=1), NT)
        return carry

    lax.fori_loop(0, cells, cell, 0)
    for g in range(groups):
        grad_ref[:, g * LANES : (g + 1) * LANES] = total_ref[g * ROWS : g * ROWS + PARAMS, :]


def call(body, out, scratch):
    return pl.pallas_call(
        body,
        out_shape=out,
        scratch_shapes=scratch,
        compiler_params=pltpu.CompilerParams(vmem_limit_bytes=48 * 1024 * 1024),
    )


def per_device(splats, target, slot_owner, slot_row, depth_order, tile_count):
    cells = lax.axis_size("cell")
    owned = splats.shape[1]
    tiles, block = slot_row.shape
    cap = max(2, 2 * tiles * block // cells)
    order = depth_order.reshape(tiles, 8, block // 8).transpose(0, 2, 1).reshape(tiles, block)
    owner = slot_owner.reshape(tiles, block)
    shape = jax.ShapeDtypeStruct
    own, pos, asking = call(
        plan_slots,
        (shape((tiles, block), I32), shape((tiles, block), I32), shape((cells, cap), I32)),
        [pltpu.VMEM((2 * cells, cap), F32)],
    )(order, owner, slot_row)
    received = lax.all_to_all(asking, "cell", split_axis=0, concat_axis=0, tiled=True)
    values = call(answer, shape((cells, ROWS, cap), F32), [])(splats, received)
    values = lax.all_to_all(values, "cell", split_axis=0, concat_axis=0, tiled=True)
    rendered, outgoing = call(
        shade,
        (shape(target.shape, F32), shape((cells, ROWS, cap), F32)),
        [pltpu.VMEM((cells * ROWS, 3 * cap), BF16)] + [pltpu.VMEM((block, PIX), F32)] * 5,
    )(values, own, pos, order, tile_count.reshape(tiles, 1), target)
    incoming = lax.all_to_all(outgoing, "cell", split_axis=0, concat_axis=0, tiled=True)
    grad_splats = call(
        collect, shape((PARAMS, owned), F32), [pltpu.VMEM((owned // LANES * ROWS, LANES), F32)]
    )(incoming, received)
    return (rendered, grad_splats)


def solution(mesh):
    in_specs = (
        P(None, "cell"),
        P(None, "cell"),
        P("cell", None, None),
        P("cell", None),
        P("cell", None),
        P("cell"),
    )
    out_specs = (P(None, "cell"), P(None, "cell"))
    return jax.shard_map(
        per_device, mesh=mesh, in_specs=in_specs, out_specs=out_specs, check_vma=False
    )
```

```python
import jax
import jax.numpy as jnp
from jax import lax
from jax.experimental import pallas as pl
from jax.experimental.pallas import tpu as pltpu
from jax.sharding import PartitionSpec as P

SIDE = 16
PIX = SIDE * SIDE
ROWS = 16
PARAMS = 9
LANES = 128
F32, BF16, I32 = jnp.float32, jnp.bfloat16, jnp.int32
NT = (((1,), (1,)), ((), ()))
TN = (((0,), (0,)), ((), ()))


def split(x, parts):
    out = []
    for part in range(parts):
        out.append(x.astype(BF16))
        if part < parts - 1:
            x = x - out[-1].astype(F32)
    return out


def dot(a, b, dims=(((1,), (0,)), ((), ()))):
    return lax.dot_general(a, b, dims, preferred_element_type=F32)


def iota(shape, axis):
    return lax.broadcasted_iota(I32, shape, axis)


def one_hot(index, count):
    return jnp.where(iota((count, index.shape[1]), 0) == index, 1.0, 0.0)


def pad_rows(pieces, count):
    have = sum(piece.shape[0] for piece in pieces)
    if have < count:
        pieces = list(pieces) + [jnp.zeros((count - have, pieces[0].shape[1]), F32)]
    return jnp.concatenate(pieces, axis=0)


def plan_slots(order_ref, owner_ref, row_ref, own_ref, pos_ref, ask_ref, parts_ref):
    tiles, block = order_ref.shape
    cells, _, cap = ask_ref.shape
    before = jnp.where(iota((block, block), 0) < iota((block, block), 1), 1.0, 0.0).astype(BF16)
    parts_ref[...] = jnp.zeros_like(parts_ref)

    def tile(t, seen):
        at = pl.ds(t, 1)
        chosen = one_hot(order_ref[at, :], block).astype(BF16)
        row = row_ref[at, :]
        source = pad_rows(
            [owner_ref[at, :].astype(F32), (row >> 8).astype(F32), (row & 255).astype(F32)], 16
        )
        moved = dot(source.astype(BF16), chosen)
        own = moved[0:1].astype(I32)
        mine = one_hot(own, cells)
        earlier = dot(mine.astype(BF16), before) + seen
        pos = jnp.sum(mine * earlier, axis=0, keepdims=True).astype(I32)
        own_ref[at, :] = own
        pos_ref[at, :] = pos
        asked = jnp.concatenate([mine * moved[1:2], mine * moved[2:3]], axis=0).astype(BF16)
        parts_ref[...] += dot(asked, one_hot(pos, cap).astype(BF16), NT)
        return seen + jnp.sum(mine, axis=1, keepdims=True)

    lax.fori_loop(0, tiles, tile, jnp.zeros((cells, 1), F32))
    both = parts_ref[...].astype(I32)
    both = both[:cells] * 256 + both[cells:]
    for c in range(cells):
        ask_ref[c] = both[c : c + 1]


def splat_table(splats_ref):
    groups = splats_ref.shape[1] // LANES
    table = jnp.concatenate(
        [pad_rows([splats_ref[:, g * LANES : (g + 1) * LANES]], ROWS) for g in range(groups)], axis=0
    )
    return jnp.concatenate(split(table, 3), axis=1)


def answer(lookup_ref, row):
    groups = lookup_ref.shape[0] // ROWS
    low = one_hot(row & (LANES - 1), LANES).astype(BF16)
    found = dot(lookup_ref[...], jnp.concatenate([low, low, low], axis=0))
    high = row // LANES
    total = jnp.zeros((ROWS, row.shape[1]), F32)
    for g in range(groups):
        total += jnp.where(high == g, found[g * ROWS : (g + 1) * ROWS], 0.0)
    return total[:PARAMS]


def scan_rows(x, keep, fill, down, combine):
    at = iota(x.shape, 0)

    def moved(y, by):
        if down:
            return jnp.where(at >= by, pltpu.roll(y, by, 0), fill)
        return jnp.where(at < 8 - by, pltpu.roll(y, 8 - by, 0), fill)

    x = moved(x, 1)
    for by in (1, 2, 4):
        x = combine(x, moved(x, by))
    return x


def shade(
    values_ref, own_ref, pos_ref, order_ref, count_ref, target_ref, rendered_ref, out_ref,
    total_ref, table_ref, f1_ref, f2_ref, alpha_ref, w_ref, h_ref,
):
    tiles, block = own_ref.shape
    cells, _, cap = values_ref.shape
    steps = block // 8
    pixel = iota((1, PIX), 1)
    x = (pixel % SIDE).astype(F32) + (0.5 - SIDE / 2)
    y = (pixel // SIDE).astype(F32) + (0.5 - SIDE / 2)
    one, zero = jnp.ones((1, PIX), F32), jnp.zeros((1, PIX), F32)
    linear = jnp.concatenate(
        [
            pad_rows([x, y, one], 8),
            pad_rows([zero, zero, zero, y, one], 8),
            pad_rows([zero, zero, zero, zero, zero, one], 8),
        ],
        axis=1,
    )
    linear = pad_rows([linear, linear, linear], 32).astype(BF16)
    moments = pad_rows([one, x, y], 16).astype(BF16)

    for c in range(cells):
        for part, piece in enumerate(split(pad_rows([values_ref[c]], ROWS), 3)):
            table_ref[c * ROWS : (c + 1) * ROWS, part * cap : (part + 1) * cap] = piece
    total_ref[...] = jnp.zeros_like(total_ref)

    def tile(t, carry):
        at = pl.ds(t, 1)
        own = own_ref[at, :]
        place = one_hot(pos_ref[at, :], cap).astype(BF16)
        found = dot(table_ref[...], jnp.concatenate([place, place, place], axis=0))
        p = jnp.zeros((ROWS, block), F32)
        for c in range(cells):
            p += jnp.where(own == c, found[c * ROWS : (c + 1) * ROWS], 0.0)
        live = jnp.where(order_ref[at, :] < count_ref[at, :], 1.0, 0.0)
        mx, my = p[0:1] - SIDE / 2, p[1:2] - SIDE / 2
        a, b, c2 = p[2:3], p[3:4], p[4:5]
        colour = p[6:9]
        sig = 1.0 / (1.0 + jnp.exp(-p[5:6]))
        unsig = 1.0 / (1.0 + jnp.exp(p[5:6]))
        factors = pad_rows([a, b, -(a * mx + b * my), c2, -(c2 * my), sig * live], 8)
        factors = pad_rows([z.astype(F32) for z in split(factors, 3)], 32).astype(BF16)
        spread = dot(factors, linear, TN)
        f1, f2 = spread[:, :PIX], spread[:, PIX : 2 * PIX]
        f1_ref[...] = f1
        f2_ref[...] = f2
        alpha_ref[...] = spread[:, 2 * PIX :] * jnp.exp(-0.5 * (f1 * f1 + f2 * f2))

        run = jnp.ones((8, PIX), F32)
        for v in range(steps):
            alpha = alpha_ref[8 * v : 8 * v + 8, :]
            w_ref[8 * v : 8 * v + 8, :] = run * alpha
            run = run * (1.0 - alpha)
        ahead = scan_rows(run, None, 1.0, True, lambda u, w: u * w)
        for v in range(steps):
            w_ref[8 * v : 8 * v + 8, :] *= ahead

        colours = [z.astype(F32) for z in split(colour, 3)]
        ch, cm, cl = colours
        wh, wl = split(w_ref[...], 2)
        stacked = pad_rows(colours, 16).astype(BF16)
        picture = dot(stacked, wh) + dot(stacked, wl)
        picture = picture[0:3] + picture[3:6] + picture[6:9]
        lanes = pl.ds(pl.multiple_of(t * PIX, PIX), PIX)
        rendered_ref[:, lanes] = picture
        error = picture - target_ref[:, lanes]
        errors = [z.astype(F32) for z in split(error, 3)]
        eh, em, el = errors
        dw = dot(
            pad_rows([ch, ch, ch, cm, cm, cl], 32).astype(BF16),
            pad_rows([eh, em, el, eh, em, eh], 32).astype(BF16),
            TN,
        )
        stacked = pad_rows(errors, 16).astype(BF16)
        dcol = dot(stacked, wh, NT) + dot(stacked, wl, NT)
        dcol = dcol[0:3] + dcol[3:6] + dcol[6:9]

        h_ref[...] = dw * w_ref[...]
        run = jnp.zeros((8, PIX), F32)
        for v in range(steps):
            run = run + h_ref[8 * v : 8 * v + 8, :]
        behind = scan_rows(run, None, 0.0, False, lambda u, w: u + w)
        for v in reversed(range(steps)):
            alpha = alpha_ref[8 * v : 8 * v + 8, :]
            u = h_ref[8 * v : 8 * v + 8, :]
            h_ref[8 * v : 8 * v + 8, :] = u - behind * (alpha / (1.0 - alpha))
            behind = behind + u

        h = h_ref[...]

        def moment(z):
            zh, zl = split(z, 2)
            return dot(moments, zh, NT) + dot(moments, zl, NT)

        m0, m1, m2 = moment(h), moment(-h * f1_ref[...]), moment(-h * f2_ref[...])
        s1, s2 = m1[0:1], m2[0:1]
        grads = pad_rows(
            [
                -a * s1,
                -b * s1 - c2 * s2,
                m1[1:2] - mx * s1,
                m1[2:3] - my * s1,
                m2[2:3] - my * s2,
                unsig * m0[0:1],
                dcol,
            ],
            ROWS,
        )
        sent = jnp.concatenate([jnp.where(own == c, grads, 0.0) for c in range(cells)], axis=0)
        sent = jnp.concatenate(split(sent, 3), axis=1)
        total_ref[...] += dot(sent, jnp.concatenate([place, place, place], axis=1), NT)
        return carry

    lax.fori_loop(0, tiles, tile, 0)
    for c in range(cells):
        out_ref[c] = total_ref[c * ROWS : c * ROWS + PARAMS, :]


def collect(part, row, total_ref):
    groups = total_ref.shape[0] // ROWS
    low = one_hot(row & (LANES - 1), LANES).astype(BF16)
    high = row // LANES
    part = pad_rows([part], ROWS)
    placed = jnp.concatenate([jnp.where(high == g, part, 0.0) for g in range(groups)], axis=0)
    placed = jnp.concatenate(split(placed, 3), axis=1)
    total_ref[...] += dot(placed, jnp.concatenate([low, low, low], axis=1), NT)


def splatting(
    splats_ref, order_ref, owner_ref, row_ref, count_ref, target_ref, rendered_ref, grad_ref,
    own_ref, pos_ref, ask_ref, asked_ref, reply_ref, values_ref, out_ref, incoming_ref,
    parts_ref, lookup_ref, sums_ref, shade_refs, send_sem, recv_sem,
):
    cells = ask_ref.shape[0]
    me = lax.axis_index("cell")
    barrier = pltpu.get_barrier_semaphore()

    def greet(step, carry):
        pl.semaphore_signal(
            barrier, inc=1, device_id=(lax.rem(me + step, cells),), device_id_type=pl.DeviceIdType.MESH
        )
        return carry

    def over_others(body):
        def one(step, carry):
            body(lax.rem(me + step, cells), lax.rem(me + cells - step, cells))
            return carry

        lax.fori_loop(1, cells, one, 0)

    def copy(phase, source_ref, landing_ref, to, slot):
        return pltpu.make_async_remote_copy(
            src_ref=source_ref.at[to],
            dst_ref=landing_ref.at[slot],
            send_sem=send_sem.at[phase, to],
            recv_sem=recv_sem.at[phase, slot],
            device_id=(to,),
            device_id_type=pl.DeviceIdType.MESH,
        )

    lax.fori_loop(1, cells, greet, 0)
    plan_slots(order_ref, owner_ref, row_ref, own_ref, pos_ref, ask_ref, parts_ref)
    pl.semaphore_wait(barrier, cells - 1)
    over_others(lambda to, source: copy(0, ask_ref, asked_ref, to, me).start())

    lookup_ref[...] = splat_table(splats_ref)
    asked_ref[me] = ask_ref[me]
    values_ref[me] = answer(lookup_ref, asked_ref[me])

    def serve(to, source):
        copy(0, ask_ref, asked_ref, source, source).wait_recv()
        reply_ref[source] = answer(lookup_ref, asked_ref[source])
        copy(1, reply_ref, values_ref, source, me).start()

    over_others(serve)
    over_others(lambda to, source: copy(1, reply_ref, values_ref, to, to).wait_recv())
    shade(
        values_ref, own_ref, pos_ref, order_ref, count_ref, target_ref, rendered_ref, out_ref,
        *shade_refs,
    )
    over_others(lambda to, source: copy(2, out_ref, incoming_ref, to, me).start())
    sums_ref[...] = jnp.zeros_like(sums_ref)
    collect(out_ref[me], asked_ref[me], sums_ref)

    def receive(to, source):
        copy(2, out_ref, incoming_ref, source, source).wait_recv()
        collect(incoming_ref[source], asked_ref[source], sums_ref)

    over_others(receive)
    for g in range(grad_ref.shape[1] // LANES):
        grad_ref[:, g * LANES : (g + 1) * LANES] = sums_ref[g * ROWS : g * ROWS + PARAMS, :]

    def finish(to, source):
        copy(0, ask_ref, asked_ref, to, me).wait_send()
        copy(1, reply_ref, values_ref, to, me).wait_send()
        copy(2, out_ref, incoming_ref, to, me).wait_send()

    over_others(finish)


def per_device(splats, target, slot_owner, slot_row, depth_order, tile_count):
    cells = lax.axis_size("cell")
    owned = splats.shape[1]
    tiles, block = slot_row.shape
    cap = max(2, 2 * tiles * block // cells)
    order = depth_order.reshape(tiles, 8, block // 8).transpose(0, 2, 1).reshape(tiles, block)
    owner = slot_owner.reshape(tiles, block)
    grouped = owned // LANES * ROWS
    vmem = pltpu.VMEM
    return pl.pallas_call(
        splatting,
        out_shape=(
            jax.ShapeDtypeStruct(target.shape, F32),
            jax.ShapeDtypeStruct((PARAMS, owned), F32),
        ),
        in_specs=[pl.BlockSpec(memory_space=pltpu.VMEM)] * 6,
        out_specs=[pl.BlockSpec(memory_space=pltpu.VMEM)] * 2,
        scratch_shapes=[
            vmem((tiles, block), I32),
            vmem((tiles, block), I32),
            vmem((cells, 1, cap), I32),
            vmem((cells, 1, cap), I32),
            vmem((cells, PARAMS, cap), F32),
            vmem((cells, PARAMS, cap), F32),
            vmem((cells, PARAMS, cap), F32),
            vmem((cells, PARAMS, cap), F32),
            vmem((2 * cells, cap), F32),
            vmem((grouped, 3 * LANES), BF16),
            vmem((grouped, LANES), F32),
            [vmem((cells * ROWS, cap), F32), vmem((cells * ROWS, 3 * cap), BF16)]
            + [vmem((block, PIX), F32)] * 5,
            pltpu.SemaphoreType.DMA((3, cells)),
            pltpu.SemaphoreType.DMA((3, cells)),
        ],
        compiler_params=pltpu.CompilerParams(
            vmem_limit_bytes=48 * 1024 * 1024, collective_id=0, has_side_effects=True
        ),
    )(splats, order, owner, slot_row, tile_count.reshape(tiles, 1), target)


def solution(mesh):
    in_specs = (
        P(None, "cell"),
        P(None, "cell"),
        P("cell", None, None),
        P("cell", None),
        P("cell", None),
        P("cell"),
    )
    out_specs = (P(None, "cell"), P(None, "cell"))
    return jax.shard_map(
        per_device, mesh=mesh, in_specs=in_specs, out_specs=out_specs, check_vma=False
    )
```

```python
import jax
import jax.numpy as jnp
from jax import lax
from jax.experimental import pallas as pl
from jax.experimental.pallas import tpu as pltpu
from jax.sharding import PartitionSpec as P

SIDE = 16
PIX = SIDE * SIDE
PARAMS = 9
LANES = 128
F32, BF16, I32 = jnp.float32, jnp.bfloat16, jnp.int32
NT = (((1,), (1,)), ((), ()))
TN = (((0,), (0,)), ((), ()))


def split(x, parts):
    out = []
    for part in range(parts):
        out.append(x.astype(BF16))
        if part < parts - 1:
            x = x - out[-1].astype(F32)
    return out


def dot(a, b, dims=(((1,), (0,)), ((), ()))):
    return lax.dot_general(a, b, dims, preferred_element_type=F32)


def iota(shape, axis):
    return lax.broadcasted_iota(I32, shape, axis)


def one_hot(index, count):
    return jnp.where(iota((count, index.shape[1]), 0) == index, 1.0, 0.0)


def pad_rows(pieces, count):
    have = sum(piece.shape[0] for piece in pieces)
    if have < count:
        pieces = list(pieces) + [jnp.zeros((count - have, pieces[0].shape[1]), F32)]
    return jnp.concatenate(pieces, axis=0)


def lockstep(works):
    works = list(works)
    while works:
        works = [work for work in works if next(work, "end") is None]


def group_of(count):
    return next(size for size in (4, 2, 1) if count % size == 0)


def gather(table, place, mask):
    found = dot(table, jnp.concatenate([place, place, place], axis=0))
    high = mask.shape[0]
    return [
        jnp.sum(found[c * high : (c + 1) * high] * mask, axis=0, keepdims=True) for c in range(PARAMS)
    ]


def scatter(rows, place, mask):
    mask = mask.astype(BF16)
    pieces = split(rows, 2)
    spread = jnp.concatenate(
        [
            jnp.concatenate([piece[c : c + 1] * mask for c in range(PARAMS)], axis=0)
            for piece in pieces
        ],
        axis=1,
    )
    return dot(spread, jnp.concatenate([place, place], axis=1), NT)


def plan_slots(order_ref, owner_ref, row_ref, own_ref, pos_ref, ask_ref, parts_ref):
    tiles, block = order_ref.shape
    cells, _, cap = ask_ref.shape
    before = jnp.where(iota((block, block), 0) < iota((block, block), 1), 1.0, 0.0).astype(BF16)
    parts_ref[...] = jnp.zeros_like(parts_ref)
    group = group_of(tiles)

    def tile(t, state, asks):
        at = pl.ds(t, 1)
        chosen = one_hot(order_ref[at, :], block).astype(BF16)
        row = row_ref[at, :]
        source = pad_rows(
            [owner_ref[at, :].astype(F32), (row >> 8).astype(F32), (row & 255).astype(F32)], 16
        )
        moved = dot(source.astype(BF16), chosen)
        yield
        own = moved[0:1].astype(I32)
        own_ref[at, :] = own
        mine = one_hot(own, cells)
        within = dot(mine.astype(BF16), before)
        asked = jnp.concatenate([mine * moved[1:2], mine * moved[2:3]], axis=0).astype(BF16)
        earlier = within + state[0]
        state[0] = state[0] + jnp.sum(mine, axis=1, keepdims=True)
        yield
        pos = jnp.sum(mine * earlier, axis=0, keepdims=True).astype(I32)
        pos_ref[at, :] = pos
        asks.append(dot(asked, one_hot(pos, cap).astype(BF16), NT))

    def some(i, seen):
        state, asks = [seen], []
        lockstep(tile(i * group + j, state, asks) for j in range(group))
        parts_ref[...] += sum(asks[1:], asks[0])
        return state[0]

    lax.fori_loop(0, tiles // group, some, jnp.zeros((cells, 1), F32))
    both = parts_ref[...].astype(I32)
    both = both[:cells] * 256 + both[cells:]
    for c in range(cells):
        ask_ref[c] = both[c : c + 1]


def splat_table(splats_ref, rows_ref):
    groups = splats_ref.shape[1] // LANES
    for c in range(PARAMS):
        for g in range(groups):
            at = c * groups + g
            rows_ref[at : at + 1, :] = splats_ref[c : c + 1, g * LANES : (g + 1) * LANES]
    return jnp.concatenate(split(rows_ref[...], 3), axis=1)


def answer(lookup_ref, row):
    low = one_hot(row & (LANES - 1), LANES).astype(BF16)
    mask = one_hot(row >> 7, lookup_ref.shape[0] // PARAMS)
    return jnp.concatenate(gather(lookup_ref[...], low, mask), axis=0)


def scan_rows(x, keep, fill, down, combine):
    at = iota(x.shape, 0)

    def moved(y, by):
        if down:
            return jnp.where(at >= by, pltpu.roll(y, by, 0), fill)
        return jnp.where(at < 8 - by, pltpu.roll(y, 8 - by, 0), fill)

    x = moved(x, 1)
    for by in (1, 2, 4):
        x = combine(x, moved(x, by))
    return x


def shade(
    values_ref, own_ref, pos_ref, order_ref, count_ref, target_ref, rendered_ref, out_ref,
    total_ref, table_ref, tile_refs,
):
    tiles, block = own_ref.shape
    cells, _, cap = values_ref.shape
    steps = block // 8
    pixel = iota((1, PIX), 1)
    x = (pixel % SIDE).astype(F32) + (0.5 - SIDE / 2)
    y = (pixel // SIDE).astype(F32) + (0.5 - SIDE / 2)
    one, zero = jnp.ones((1, PIX), F32), jnp.zeros((1, PIX), F32)
    linear = jnp.concatenate(
        [
            pad_rows([x, y, one], 8),
            pad_rows([zero, zero, zero, y, one], 8),
            pad_rows([zero, zero, zero, zero, zero, one], 8),
        ],
        axis=1,
    )
    linear = pad_rows([linear, linear, linear], 32).astype(BF16)
    moments = pad_rows([one, x, y], 16).astype(BF16)

    for c in range(PARAMS):
        for part, piece in enumerate(split(values_ref[:, c, :], 3)):
            table_ref[c * cells : (c + 1) * cells, part * cap : (part + 1) * cap] = piece
    total_ref[...] = jnp.zeros_like(total_ref)

    def tile(t, refs, puts):
        f1_ref, f2_ref, alpha_ref, w_ref, h_ref = refs
        at = pl.ds(t, 1)
        own = own_ref[at, :]
        place = one_hot(pos_ref[at, :], cap).astype(BF16)
        mine = one_hot(own, cells)
        p = gather(table_ref[...], place, mine)
        yield
        live = jnp.where(order_ref[at, :] < count_ref[at, :], 1.0, 0.0)
        mx, my = p[0] - SIDE / 2, p[1] - SIDE / 2
        a, b, c2 = p[2], p[3], p[4]
        colour = jnp.concatenate(p[6:9], axis=0)
        sig = 1.0 / (1.0 + jnp.exp(-p[5]))
        unsig = 1.0 / (1.0 + jnp.exp(p[5]))
        factors = pad_rows([a, b, -(a * mx + b * my), c2, -(c2 * my), sig * live], 8)
        factors = pad_rows([z.astype(F32) for z in split(factors, 3)], 32).astype(BF16)
        spread = dot(factors, linear, TN)
        yield
        f1, f2 = spread[:, :PIX], spread[:, PIX : 2 * PIX]
        f1_ref[...] = f1
        f2_ref[...] = f2
        alpha_ref[...] = spread[:, 2 * PIX :] * jnp.exp(-0.5 * (f1 * f1 + f2 * f2))

        yield
        run = jnp.ones((8, PIX), F32)
        for v in range(steps):
            alpha = alpha_ref[8 * v : 8 * v + 8, :]
            w_ref[8 * v : 8 * v + 8, :] = run * alpha
            run = run * (1.0 - alpha)
        ahead = scan_rows(run, None, 1.0, True, lambda u, w: u * w)
        for v in range(steps):
            w_ref[8 * v : 8 * v + 8, :] *= ahead

        yield
        colours = [z.astype(F32) for z in split(colour, 3)]
        ch, cm, cl = colours
        wh, wl = split(w_ref[...], 2)
        stacked = pad_rows(colours, 16).astype(BF16)
        picture = dot(stacked, wh) + dot(stacked, wl)
        yield
        picture = picture[0:3] + picture[3:6] + picture[6:9]
        lanes = pl.ds(pl.multiple_of(t * PIX, PIX), PIX)
        rendered_ref[:, lanes] = picture
        error = picture - target_ref[:, lanes]
        errors = [z.astype(F32) for z in split(error, 3)]
        eh, em, el = errors
        dw = dot(
            pad_rows([ch, ch, ch, cm, cm, cl], 32).astype(BF16),
            pad_rows([eh, em, el, eh, em, eh], 32).astype(BF16),
            TN,
        )
        stacked = pad_rows(errors, 16).astype(BF16)
        dcol = dot(stacked, wh, NT) + dot(stacked, wl, NT)
        yield
        dcol = dcol[0:3] + dcol[3:6] + dcol[6:9]

        h_ref[...] = dw * w_ref[...]
        run = jnp.zeros((8, PIX), F32)
        for v in range(steps):
            run = run + h_ref[8 * v : 8 * v + 8, :]
        behind = scan_rows(run, None, 0.0, False, lambda u, w: u + w)
        for v in reversed(range(steps)):
            alpha = alpha_ref[8 * v : 8 * v + 8, :]
            u = h_ref[8 * v : 8 * v + 8, :]
            h_ref[8 * v : 8 * v + 8, :] = u - behind * (alpha / (1.0 - alpha))
            behind = behind + u

        yield
        h = h_ref[...]

        def moment(z):
            zh, zl = split(z, 2)
            return dot(moments, zh, NT) + dot(moments, zl, NT)

        m0, m1, m2 = moment(h), moment(-h * f1_ref[...]), moment(-h * f2_ref[...])
        yield
        s1, s2 = m1[0:1], m2[0:1]
        grads = pad_rows(
            [
                -a * s1,
                -b * s1 - c2 * s2,
                m1[1:2] - mx * s1,
                m1[2:3] - my * s1,
                m2[2:3] - my * s2,
                unsig * m0[0:1],
                dcol,
            ],
            PARAMS,
        )
        puts.append(scatter(grads, place, mine))

    group = len(tile_refs)

    def some(i, carry):
        puts = []
        lockstep(tile(i * group + j, tile_refs[j], puts) for j in range(group))
        total_ref[...] += sum(puts[1:], puts[0])
        return carry

    lax.fori_loop(0, tiles // group, some, 0)
    for c in range(PARAMS):
        out_ref[:, c, :] = total_ref[c * cells : (c + 1) * cells, :]


def collect(part, row, groups):
    low = one_hot(row & (LANES - 1), LANES).astype(BF16)
    return scatter(part, low, one_hot(row >> 7, groups))


def splatting(
    splats_ref, order_ref, owner_ref, row_ref, count_ref, target_ref, rendered_ref, grad_ref,
    own_ref, pos_ref, ask_ref, asked_ref, reply_ref, values_ref, out_ref, incoming_ref,
    parts_ref, lookup_ref, sums_ref, shade_refs, send_sem, recv_sem,
):
    cells = ask_ref.shape[0]
    me = lax.axis_index("cell")
    barrier = pltpu.get_barrier_semaphore()

    def greet(step, carry):
        pl.semaphore_signal(
            barrier, inc=1, device_id=(lax.rem(me + step, cells),), device_id_type=pl.DeviceIdType.MESH
        )
        return carry

    def over_others(body):
        def one(step, carry):
            body(lax.rem(me + step, cells), lax.rem(me + cells - step, cells))
            return carry

        lax.fori_loop(1, cells, one, 0)

    def copy(phase, source_ref, landing_ref, to, slot):
        return pltpu.make_async_remote_copy(
            src_ref=source_ref.at[to],
            dst_ref=landing_ref.at[slot],
            send_sem=send_sem.at[phase, to],
            recv_sem=recv_sem.at[phase, slot],
            device_id=(to,),
            device_id_type=pl.DeviceIdType.MESH,
        )

    lax.fori_loop(1, cells, greet, 0)
    plan_slots(order_ref, owner_ref, row_ref, own_ref, pos_ref, ask_ref, parts_ref)
    lookup_ref[...] = splat_table(splats_ref, sums_ref)
    pl.semaphore_wait(barrier, cells - 1)
    over_others(lambda to, source: copy(0, ask_ref, asked_ref, to, me).start())

    def in_groups(body):
        size = group_of(cells)
        body([0] + list(range(1, size)), True)

        def one(i, carry):
            body([i * size + j for j in range(size)], False)
            return carry

        lax.fori_loop(1, cells // size, one, 0)

    def source_at(step):
        return lax.rem(me + cells - step, cells)

    def serve(steps, first):
        sources = [source_at(step) for step in steps]
        if first:
            asked_ref[me] = ask_ref[me]
        for source in sources[1 if first else 0 :]:
            copy(0, ask_ref, asked_ref, source, source).wait_recv()
        replies = [answer(lookup_ref, asked_ref[source]) for source in sources]
        if first:
            values_ref[me] = replies[0]
        for source, reply in list(zip(sources, replies))[1 if first else 0 :]:
            reply_ref[source] = reply
            copy(1, reply_ref, values_ref, source, me).start()

    in_groups(serve)
    over_others(lambda to, source: copy(1, reply_ref, values_ref, to, to).wait_recv())
    shade(
        values_ref, own_ref, pos_ref, order_ref, count_ref, target_ref, rendered_ref, out_ref,
        *shade_refs,
    )
    over_others(lambda to, source: copy(2, out_ref, incoming_ref, to, me).start())
    sums_ref[...] = jnp.zeros_like(sums_ref)
    groups = sums_ref.shape[0] // PARAMS

    def receive(steps, first):
        sources = [source_at(step) for step in steps]
        for source in sources[1 if first else 0 :]:
            copy(2, out_ref, incoming_ref, source, source).wait_recv()
        parts = [incoming_ref[source] for source in sources[1 if first else 0 :]]
        if first:
            parts = [out_ref[me]] + parts
        added = [collect(part, asked_ref[source], groups) for part, source in zip(parts, sources)]
        sums_ref[...] += sum(added[1:], added[0])

    in_groups(receive)
    grad_ref[...] = sums_ref[...]

    def finish(to, source):
        copy(0, ask_ref, asked_ref, to, me).wait_send()
        copy(1, reply_ref, values_ref, to, me).wait_send()
        copy(2, out_ref, incoming_ref, to, me).wait_send()

    over_others(finish)


def per_device(splats, target, slot_owner, slot_row, depth_order, tile_count):
    cells = lax.axis_size("cell")
    owned = splats.shape[1]
    tiles, block = slot_row.shape
    cap = max(2, 2 * tiles * block // cells)
    order = depth_order.reshape(tiles, 8, block // 8).transpose(0, 2, 1).reshape(tiles, block)
    owner = slot_owner.reshape(tiles, block)
    grouped = PARAMS * (owned // LANES)
    pair = 2 if tiles % 2 == 0 else 1
    vmem = pltpu.VMEM
    rendered, grad = pl.pallas_call(
        splatting,
        out_shape=(
            jax.ShapeDtypeStruct(target.shape, F32),
            jax.ShapeDtypeStruct((grouped, LANES), F32),
        ),
        in_specs=[pl.BlockSpec(memory_space=pltpu.VMEM)] * 6,
        out_specs=[pl.BlockSpec(memory_space=pltpu.VMEM)] * 2,
        scratch_shapes=[
            vmem((tiles, block), I32),
            vmem((tiles, block), I32),
            vmem((cells, 1, cap), I32),
            vmem((cells, 1, cap), I32),
            vmem((cells, PARAMS, cap), F32),
            vmem((cells, PARAMS, cap), F32),
            vmem((cells, PARAMS, cap), F32),
            vmem((cells, PARAMS, cap), F32),
            vmem((2 * cells, cap), F32),
            vmem((grouped, 3 * LANES), BF16),
            vmem((grouped, LANES), F32),
            [
                vmem((PARAMS * cells, cap), F32),
                vmem((PARAMS * cells, 3 * cap), BF16),
                [[vmem((block, PIX), F32)] * 5] * pair,
            ],
            pltpu.SemaphoreType.DMA((3, cells)),
            pltpu.SemaphoreType.DMA((3, cells)),
        ],
        compiler_params=pltpu.CompilerParams(
            vmem_limit_bytes=48 * 1024 * 1024, collective_id=0, has_side_effects=True
        ),
    )(splats, order, owner, slot_row, tile_count.reshape(tiles, 1), target)
    return (rendered, grad.reshape(PARAMS, owned))


def solution(mesh):
    in_specs = (
        P(None, "cell"),
        P(None, "cell"),
        P("cell", None, None),
        P("cell", None),
        P("cell", None),
        P("cell"),
    )
    out_specs = (P(None, "cell"), P(None, "cell"))
    return jax.shard_map(
        per_device, mesh=mesh, in_specs=in_specs, out_specs=out_specs, check_vma=False
    )
```

```python
import jax
import jax.numpy as jnp
from jax import lax
from jax.experimental import pallas as pl
from jax.experimental.pallas import tpu as pltpu
from jax.sharding import PartitionSpec as P

SIDE = 16
PIX = SIDE * SIDE
PARAMS = 9
LANES = 128
F32, BF16, I32 = jnp.float32, jnp.bfloat16, jnp.int32
NT = (((1,), (1,)), ((), ()))
TN = (((0,), (0,)), ((), ()))


def split(x, parts):
    out = []
    for part in range(parts):
        out.append(x.astype(BF16))
        if part < parts - 1:
            x = x - out[-1].astype(F32)
    return out


def dot(a, b, dims=(((1,), (0,)), ((), ()))):
    return lax.dot_general(a, b, dims, preferred_element_type=F32)


def iota(shape, axis):
    return lax.broadcasted_iota(I32, shape, axis)


def one_hot(index, count):
    return jnp.where(iota((count, index.shape[1]), 0) == index, 1.0, 0.0)


def pad_rows(pieces, count):
    have = sum(piece.shape[0] for piece in pieces)
    if have < count:
        pieces = list(pieces) + [jnp.zeros((count - have, pieces[0].shape[1]), F32)]
    return jnp.concatenate(pieces, axis=0)


def lockstep(works):
    works = list(works)
    while works:
        works = [work for work in works if next(work, "end") is None]


def group_of(count):
    return next(size for size in (4, 2, 1) if count % size == 0)


def gather(table, place, mask):
    found = dot(table, jnp.concatenate([place, place, place], axis=0))
    high = mask.shape[0]
    return [
        jnp.sum(found[c * high : (c + 1) * high] * mask, axis=0, keepdims=True) for c in range(PARAMS)
    ]


def scatter(rows, place, mask):
    mask = mask.astype(BF16)
    pieces = split(rows, 2)
    spread = jnp.concatenate(
        [
            jnp.concatenate([piece[c : c + 1] * mask for c in range(PARAMS)], axis=0)
            for piece in pieces
        ],
        axis=1,
    )
    return dot(spread, jnp.concatenate([place, place], axis=1), NT)


def plan_slots(depth_ref, order_ref, owner_ref, row_ref, own_ref, pos_ref, ask_ref, parts_ref):
    tiles, block = order_ref.shape
    cells, _, cap = ask_ref.shape
    slot, place = iota((block, block), 0), iota((block, block), 1)
    strided = jnp.where(slot == (place & 7) * (block // 8) + (place >> 3), 1.0, 0.0).astype(BF16)
    order_ref[...] = dot(depth_ref[...].astype(F32).astype(BF16), strided).astype(I32)
    before = jnp.where(iota((block, block), 0) < iota((block, block), 1), 1.0, 0.0).astype(BF16)
    parts_ref[...] = jnp.zeros_like(parts_ref)
    group = group_of(tiles)

    def tile(t, state, asks):
        at = pl.ds(t, 1)
        chosen = one_hot(order_ref[at, :], block).astype(BF16)
        row = row_ref[at, :]
        source = pad_rows(
            [owner_ref[at, :].astype(F32), (row >> 8).astype(F32), (row & 255).astype(F32)], 16
        )
        moved = dot(source.astype(BF16), chosen)
        yield
        own = moved[0:1].astype(I32)
        own_ref[at, :] = own
        mine = one_hot(own, cells)
        within = dot(mine.astype(BF16), before)
        asked = jnp.concatenate([mine * moved[1:2], mine * moved[2:3]], axis=0).astype(BF16)
        earlier = within + state[0]
        state[0] = state[0] + jnp.sum(mine, axis=1, keepdims=True)
        yield
        pos = jnp.sum(mine * earlier, axis=0, keepdims=True).astype(I32)
        pos_ref[at, :] = pos
        asks.append(dot(asked, one_hot(pos, cap).astype(BF16), NT))

    def some(i, seen):
        state, asks = [seen], []
        lockstep(tile(i * group + j, state, asks) for j in range(group))
        parts_ref[...] += sum(asks[1:], asks[0])
        return state[0]

    lax.fori_loop(0, tiles // group, some, jnp.zeros((cells, 1), F32))
    both = parts_ref[...].astype(I32)
    both = both[:cells] * 256 + both[cells:]
    for c in range(cells):
        ask_ref[c] = both[c : c + 1]


def splat_table(splats_ref, rows_ref):
    groups = splats_ref.shape[1] // LANES
    for c in range(PARAMS):
        for g in range(groups):
            at = c * groups + g
            rows_ref[at : at + 1, :] = splats_ref[c : c + 1, g * LANES : (g + 1) * LANES]
    return jnp.concatenate(split(rows_ref[...], 3), axis=1)


def answer(lookup_ref, row):
    low = one_hot(row & (LANES - 1), LANES).astype(BF16)
    mask = one_hot(row >> 7, lookup_ref.shape[0] // PARAMS)
    return jnp.concatenate(gather(lookup_ref[...], low, mask), axis=0)


def scan_rows(x, keep, fill, down, combine):
    at = iota(x.shape, 0)

    def moved(y, by):
        if down:
            return jnp.where(at >= by, pltpu.roll(y, by, 0), fill)
        return jnp.where(at < 8 - by, pltpu.roll(y, 8 - by, 0), fill)

    x = moved(x, 1)
    for by in (1, 2, 4):
        x = combine(x, moved(x, by))
    return x


def shade(
    values_ref, own_ref, pos_ref, order_ref, count_ref, target_ref, rendered_ref, out_ref,
    total_ref, table_ref, tile_refs,
):
    tiles, block = own_ref.shape
    cells, _, cap = values_ref.shape
    steps = block // 8
    pixel = iota((1, PIX), 1)
    x = (pixel % SIDE).astype(F32) + (0.5 - SIDE / 2)
    y = (pixel // SIDE).astype(F32) + (0.5 - SIDE / 2)
    one, zero = jnp.ones((1, PIX), F32), jnp.zeros((1, PIX), F32)
    linear = jnp.concatenate(
        [
            pad_rows([x, y, one], 8),
            pad_rows([zero, zero, zero, y, one], 8),
            pad_rows([zero, zero, zero, zero, zero, one], 8),
        ],
        axis=1,
    )
    linear = pad_rows([linear, linear, linear], 32).astype(BF16)
    moments = pad_rows([one, x, y], 16).astype(BF16)

    for c in range(PARAMS):
        for part, piece in enumerate(split(values_ref[:, c, :], 3)):
            table_ref[c * cells : (c + 1) * cells, part * cap : (part + 1) * cap] = piece
    total_ref[...] = jnp.zeros_like(total_ref)

    def tile(t, refs, puts):
        f1_ref, f2_ref, alpha_ref, w_ref, h_ref = refs
        at = pl.ds(t, 1)
        own = own_ref[at, :]
        place = one_hot(pos_ref[at, :], cap).astype(BF16)
        mine = one_hot(own, cells)
        p = gather(table_ref[...], place, mine)
        yield
        live = jnp.where(order_ref[at, :] < count_ref[at, :], 1.0, 0.0)
        mx, my = p[0] - SIDE / 2, p[1] - SIDE / 2
        a, b, c2 = p[2], p[3], p[4]
        colour = jnp.concatenate(p[6:9], axis=0)
        sig = 1.0 / (1.0 + jnp.exp(-p[5]))
        unsig = 1.0 / (1.0 + jnp.exp(p[5]))
        factors = pad_rows([a, b, -(a * mx + b * my), c2, -(c2 * my), sig * live], 8)
        factors = pad_rows([z.astype(F32) for z in split(factors, 3)], 32).astype(BF16)
        spread = dot(factors, linear, TN)
        yield
        f1, f2 = spread[:, :PIX], spread[:, PIX : 2 * PIX]
        f1_ref[...] = f1
        f2_ref[...] = f2
        alpha_ref[...] = spread[:, 2 * PIX :] * jnp.exp(-0.5 * (f1 * f1 + f2 * f2))

        yield
        run = jnp.ones((8, PIX), F32)
        for v in range(steps):
            alpha = alpha_ref[8 * v : 8 * v + 8, :]
            w_ref[8 * v : 8 * v + 8, :] = run * alpha
            run = run * (1.0 - alpha)
        ahead = scan_rows(run, None, 1.0, True, lambda u, w: u * w)
        for v in range(steps):
            w_ref[8 * v : 8 * v + 8, :] *= ahead

        yield
        colours = [z.astype(F32) for z in split(colour, 3)]
        ch, cm, cl = colours
        wh, wl = split(w_ref[...], 2)
        stacked = pad_rows(colours, 16).astype(BF16)
        picture = dot(stacked, wh) + dot(stacked, wl)
        yield
        picture = picture[0:3] + picture[3:6] + picture[6:9]
        lanes = pl.ds(pl.multiple_of(t * PIX, PIX), PIX)
        rendered_ref[:, lanes] = picture
        error = picture - target_ref[:, lanes]
        errors = [z.astype(F32) for z in split(error, 3)]
        eh, em, el = errors
        dw = dot(
            pad_rows([ch, ch, ch, cm, cm, cl], 32).astype(BF16),
            pad_rows([eh, em, el, eh, em, eh], 32).astype(BF16),
            TN,
        )
        stacked = pad_rows(errors, 16).astype(BF16)
        dcol = dot(stacked, wh, NT) + dot(stacked, wl, NT)
        yield
        dcol = dcol[0:3] + dcol[3:6] + dcol[6:9]

        h_ref[...] = dw * w_ref[...]
        run = jnp.zeros((8, PIX), F32)
        for v in range(steps):
            run = run + h_ref[8 * v : 8 * v + 8, :]
        behind = scan_rows(run, None, 0.0, False, lambda u, w: u + w)
        for v in reversed(range(steps)):
            alpha = alpha_ref[8 * v : 8 * v + 8, :]
            u = h_ref[8 * v : 8 * v + 8, :]
            h_ref[8 * v : 8 * v + 8, :] = u - behind * (alpha / (1.0 - alpha))
            behind = behind + u

        yield
        h = h_ref[...]

        def moment(z):
            zh, zl = split(z, 2)
            return dot(moments, zh, NT) + dot(moments, zl, NT)

        m0, m1, m2 = moment(h), moment(-h * f1_ref[...]), moment(-h * f2_ref[...])
        yield
        s1, s2 = m1[0:1], m2[0:1]
        grads = pad_rows(
            [
                -a * s1,
                -b * s1 - c2 * s2,
                m1[1:2] - mx * s1,
                m1[2:3] - my * s1,
                m2[2:3] - my * s2,
                unsig * m0[0:1],
                dcol,
            ],
            PARAMS,
        )
        puts.append(scatter(grads, place, mine))

    group = len(tile_refs)

    def some(i, carry):
        puts = []
        lockstep(tile(i * group + j, tile_refs[j], puts) for j in range(group))
        total_ref[...] += sum(puts[1:], puts[0])
        return carry

    lax.fori_loop(0, tiles // group, some, 0)
    for c in range(PARAMS):
        out_ref[:, c, :] = total_ref[c * cells : (c + 1) * cells, :]


def collect(part, row, groups):
    low = one_hot(row & (LANES - 1), LANES).astype(BF16)
    return scatter(part, low, one_hot(row >> 7, groups))


def splatting(
    splats_ref, depth_ref, owner_ref, row_ref, count_ref, target_ref, rendered_ref, grad_ref,
    order_ref, own_ref, pos_ref, ask_ref, asked_ref, reply_ref, values_ref, out_ref, incoming_ref,
    parts_ref, lookup_ref, sums_ref, shade_refs, send_sem, recv_sem,
):
    cells = ask_ref.shape[0]
    me = lax.axis_index("cell")
    barrier = pltpu.get_barrier_semaphore()

    def greet(step, carry):
        pl.semaphore_signal(
            barrier, inc=1, device_id=(lax.rem(me + step, cells),), device_id_type=pl.DeviceIdType.MESH
        )
        return carry

    def over_others(body):
        def one(step, carry):
            body(lax.rem(me + step, cells), lax.rem(me + cells - step, cells))
            return carry

        lax.fori_loop(1, cells, one, 0)

    def copy(phase, source_ref, landing_ref, to, slot):
        return pltpu.make_async_remote_copy(
            src_ref=source_ref.at[to],
            dst_ref=landing_ref.at[slot],
            send_sem=send_sem.at[phase, to],
            recv_sem=recv_sem.at[phase, slot],
            device_id=(to,),
            device_id_type=pl.DeviceIdType.MESH,
        )

    lax.fori_loop(1, cells, greet, 0)
    plan_slots(depth_ref, order_ref, owner_ref, row_ref, own_ref, pos_ref, ask_ref, parts_ref)
    lookup_ref[...] = splat_table(splats_ref, sums_ref)
    pl.semaphore_wait(barrier, cells - 1)
    over_others(lambda to, source: copy(0, ask_ref, asked_ref, to, me).start())

    def in_groups(body):
        size = group_of(cells)
        body([0] + list(range(1, size)), True)

        def one(i, carry):
            body([i * size + j for j in range(size)], False)
            return carry

        lax.fori_loop(1, cells // size, one, 0)

    def source_at(step):
        return lax.rem(me + cells - step, cells)

    def serve(steps, first):
        sources = [source_at(step) for step in steps]
        if first:
            asked_ref[me] = ask_ref[me]
        for source in sources[1 if first else 0 :]:
            copy(0, ask_ref, asked_ref, source, source).wait_recv()
        replies = [answer(lookup_ref, asked_ref[source]) for source in sources]
        if first:
            values_ref[me] = replies[0]
        for source, reply in list(zip(sources, replies))[1 if first else 0 :]:
            reply_ref[source] = reply
            copy(1, reply_ref, values_ref, source, me).start()

    in_groups(serve)
    over_others(lambda to, source: copy(0, ask_ref, asked_ref, to, me).wait_send())
    over_others(lambda to, source: copy(1, reply_ref, values_ref, source, source).wait_recv())
    shade(
        values_ref, own_ref, pos_ref, order_ref, count_ref, target_ref, rendered_ref, out_ref,
        *shade_refs,
    )
    over_others(lambda to, source: copy(2, out_ref, incoming_ref, to, me).start())
    sums_ref[...] = jnp.zeros_like(sums_ref)
    over_others(lambda to, source: copy(1, reply_ref, values_ref, to, me).wait_send())
    groups = sums_ref.shape[0] // PARAMS

    def receive(steps, first):
        sources = [source_at(step) for step in steps]
        for source in sources[1 if first else 0 :]:
            copy(2, out_ref, incoming_ref, source, source).wait_recv()
        parts = [incoming_ref[source] for source in sources[1 if first else 0 :]]
        if first:
            parts = [out_ref[me]] + parts
        added = [collect(part, asked_ref[source], groups) for part, source in zip(parts, sources)]
        sums_ref[...] += sum(added[1:], added[0])

    in_groups(receive)
    grad_ref[...] = sums_ref[...]

    over_others(lambda to, source: copy(2, out_ref, incoming_ref, to, me).wait_send())


def per_device(splats, target, slot_owner, slot_row, depth_order, tile_count):
    cells = lax.axis_size("cell")
    owned = splats.shape[1]
    tiles, block = slot_row.shape
    cap = max(2, 2 * tiles * block // cells)
    owner = slot_owner.reshape(tiles, block)
    grouped = PARAMS * (owned // LANES)
    vmem = pltpu.VMEM
    rendered, grad = pl.pallas_call(
        splatting,
        out_shape=(
            jax.ShapeDtypeStruct(target.shape, F32),
            jax.ShapeDtypeStruct((grouped, LANES), F32),
        ),
        in_specs=[pl.BlockSpec(memory_space=pltpu.VMEM)] * 6,
        out_specs=[pl.BlockSpec(memory_space=pltpu.VMEM)] * 2,
        scratch_shapes=[
            vmem((tiles, block), I32),
            vmem((tiles, block), I32),
            vmem((tiles, block), I32),
            vmem((cells, 1, cap), I32),
            vmem((cells, 1, cap), I32),
            vmem((cells, PARAMS, cap), F32),
            vmem((cells, PARAMS, cap), F32),
            vmem((cells, PARAMS, cap), F32),
            vmem((cells, PARAMS, cap), F32),
            vmem((2 * cells, cap), F32),
            vmem((grouped, 3 * LANES), BF16),
            vmem((grouped, LANES), F32),
            [
                vmem((PARAMS * cells, cap), F32),
                vmem((PARAMS * cells, 3 * cap), BF16),
                [[vmem((block, PIX), F32)] * 5] * group_of(tiles),
            ],
            pltpu.SemaphoreType.DMA((3, cells)),
            pltpu.SemaphoreType.DMA((3, cells)),
        ],
        compiler_params=pltpu.CompilerParams(
            vmem_limit_bytes=48 * 1024 * 1024, collective_id=0, has_side_effects=True
        ),
    )(splats, depth_order, owner, slot_row, tile_count.reshape(tiles, 1), target)
    return (rendered, grad.reshape(PARAMS, owned))


def solution(mesh):
    in_specs = (
        P(None, "cell"),
        P(None, "cell"),
        P("cell", None, None),
        P("cell", None),
        P("cell", None),
        P("cell"),
    )
    out_specs = (P(None, "cell"), P(None, "cell"))
    return jax.shard_map(
        per_device, mesh=mesh, in_specs=in_specs, out_specs=out_specs, check_vma=False
    )
```

```python
import jax
import jax.numpy as jnp
from jax import lax
from jax.experimental import pallas as pl
from jax.experimental.pallas import tpu as pltpu
from jax.sharding import PartitionSpec as P

SIDE = 16
PIX = SIDE * SIDE
PARAMS = 9
LANES = 128
F32, BF16, I32 = jnp.float32, jnp.bfloat16, jnp.int32
NT = (((1,), (1,)), ((), ()))
TN = (((0,), (0,)), ((), ()))


def split(x, parts):
    out = []
    for part in range(parts):
        out.append(x.astype(BF16))
        if part < parts - 1:
            x = x - out[-1].astype(F32)
    return out


def dot(a, b, dims=(((1,), (0,)), ((), ()))):
    return lax.dot_general(a, b, dims, preferred_element_type=F32)


def iota(shape, axis):
    return lax.broadcasted_iota(I32, shape, axis)


def one_hot(index, count):
    return jnp.where(iota((count, index.shape[1]), 0) == index, 1.0, 0.0)


def inverse(x):
    guess = pl.reciprocal(x, approx=True)
    return guess * (2.0 - x * guess)


def pad_rows(pieces, count):
    have = sum(piece.shape[0] for piece in pieces)
    if have < count:
        pieces = list(pieces) + [jnp.zeros((count - have, pieces[0].shape[1]), F32)]
    return jnp.concatenate(pieces, axis=0)


def lockstep(works):
    works = list(works)
    while works:
        works = [work for work in works if next(work, "end") is None]


def group_of(count, most):
    return next(size for size in range(most, 0, -1) if count % size == 0)


def gather(table, place, mask):
    found = dot(table, jnp.concatenate([place, place, place], axis=0))
    high = mask.shape[0]
    return [
        jnp.sum(found[c * high : (c + 1) * high] * mask, axis=0, keepdims=True) for c in range(PARAMS)
    ]


def scatter(rows, place, mask):
    mask = mask.astype(BF16)
    pieces = split(rows, 2)
    spread = jnp.concatenate(
        [
            jnp.concatenate([piece[c : c + 1] * mask for c in range(PARAMS)], axis=0)
            for piece in pieces
        ],
        axis=1,
    )
    return dot(spread, jnp.concatenate([place, place], axis=1), NT)


def plan_slots(depth_ref, order_ref, owner_ref, row_ref, own_ref, pos_ref, ask_ref, parts_ref):
    tiles, block = order_ref.shape
    cells, _, cap = ask_ref.shape
    slot, place = iota((block, block), 0), iota((block, block), 1)
    strided = jnp.where(slot == (place & 7) * (block // 8) + (place >> 3), 1.0, 0.0).astype(BF16)
    order_ref[...] = dot(depth_ref[...].astype(F32).astype(BF16), strided).astype(I32)
    before = jnp.where(iota((block, block), 0) < iota((block, block), 1), 1.0, 0.0).astype(BF16)
    parts_ref[...] = jnp.zeros_like(parts_ref)
    group = group_of(tiles, 8)

    def tile(t, state, asks):
        at = pl.ds(t, 1)
        chosen = one_hot(order_ref[at, :], block).astype(BF16)
        row = row_ref[at, :]
        source = pad_rows(
            [owner_ref[at, :].astype(F32), (row >> 8).astype(F32), (row & 255).astype(F32)], 16
        )
        moved = dot(source.astype(BF16), chosen)
        yield
        own = moved[0:1].astype(I32)
        own_ref[at, :] = own
        mine = one_hot(own, cells)
        within = dot(mine.astype(BF16), before)
        asked = jnp.concatenate([mine * moved[1:2], mine * moved[2:3]], axis=0).astype(BF16)
        earlier = within + state[0]
        state[0] = state[0] + jnp.sum(mine, axis=1, keepdims=True)
        yield
        pos = jnp.sum(mine * earlier, axis=0, keepdims=True).astype(I32)
        pos_ref[at, :] = pos
        asks.append(dot(asked, one_hot(pos, cap).astype(BF16), NT))

    def some(i, seen):
        state, asks = [seen], []
        lockstep(tile(i * group + j, state, asks) for j in range(group))
        parts_ref[...] += sum(asks[1:], asks[0])
        return state[0]

    lax.fori_loop(0, tiles // group, some, jnp.zeros((cells, 1), F32))
    both = parts_ref[...].astype(I32)
    both = both[:cells] * 256 + both[cells:]
    for c in range(cells):
        ask_ref[c] = both[c : c + 1]


def splat_table(splats_ref, rows_ref):
    groups = splats_ref.shape[1] // LANES
    for c in range(PARAMS):
        for g in range(groups):
            at = c * groups + g
            rows_ref[at : at + 1, :] = splats_ref[c : c + 1, g * LANES : (g + 1) * LANES]
    return jnp.concatenate(split(rows_ref[...], 3), axis=1)


def answer(lookup_ref, row):
    low = one_hot(row & (LANES - 1), LANES).astype(BF16)
    mask = one_hot(row >> 7, lookup_ref.shape[0] // PARAMS)
    return jnp.concatenate(gather(lookup_ref[...], low, mask), axis=0)


def scan_rows(x, keep, fill, down, combine):
    at = iota(x.shape, 0)

    def moved(y, by):
        if down:
            return jnp.where(at >= by, pltpu.roll(y, by, 0), fill)
        return jnp.where(at < 8 - by, pltpu.roll(y, 8 - by, 0), fill)

    x = moved(x, 1)
    for by in (1, 2, 4):
        x = combine(x, moved(x, by))
    return x


def shade(
    values_ref, own_ref, pos_ref, order_ref, count_ref, target_ref, rendered_ref, out_ref,
    total_ref, table_ref, tile_refs,
):
    tiles, block = own_ref.shape
    cells, _, cap = values_ref.shape
    steps = block // 8
    pixel = iota((1, PIX), 1)
    x = (pixel % SIDE).astype(F32) + (0.5 - SIDE / 2)
    y = (pixel // SIDE).astype(F32) + (0.5 - SIDE / 2)
    one, zero = jnp.ones((1, PIX), F32), jnp.zeros((1, PIX), F32)
    linear = jnp.concatenate(
        [
            pad_rows([x, y, one], 8),
            pad_rows([zero, zero, zero, y, one], 8),
            pad_rows([zero, zero, zero, zero, zero, one], 8),
        ],
        axis=1,
    )
    linear = pad_rows([linear, linear, linear], 32).astype(BF16)
    moments = pad_rows([one, x, y], 16).astype(BF16)

    for c in range(PARAMS):
        for part, piece in enumerate(split(values_ref[:, c, :], 3)):
            table_ref[c * cells : (c + 1) * cells, part * cap : (part + 1) * cap] = piece
    total_ref[...] = jnp.zeros_like(total_ref)

    def tile(t, refs, puts):
        f1_ref, f2_ref, alpha_ref, w_ref, h_ref = refs
        at = pl.ds(t, 1)
        own = own_ref[at, :]
        place = one_hot(pos_ref[at, :], cap).astype(BF16)
        mine = one_hot(own, cells)
        p = gather(table_ref[...], place, mine)
        yield
        live = jnp.where(order_ref[at, :] < count_ref[at, :], 1.0, 0.0)
        mx, my = p[0] - SIDE / 2, p[1] - SIDE / 2
        a, b, c2 = p[2], p[3], p[4]
        colour = jnp.concatenate(p[6:9], axis=0)
        sig = 1.0 / (1.0 + jnp.exp(-p[5]))
        unsig = 1.0 / (1.0 + jnp.exp(p[5]))
        factors = pad_rows([a, b, -(a * mx + b * my), c2, -(c2 * my), sig * live], 8)
        factors = pad_rows([z.astype(F32) for z in split(factors, 3)], 32).astype(BF16)
        spread = dot(factors, linear, TN)
        yield
        f1, f2 = spread[:, :PIX], spread[:, PIX : 2 * PIX]
        f1_ref[...] = f1
        f2_ref[...] = f2
        alpha_ref[...] = spread[:, 2 * PIX :] * jnp.exp(-0.5 * (f1 * f1 + f2 * f2))

        yield
        run = jnp.ones((8, PIX), F32)
        for v in range(steps):
            alpha = alpha_ref[8 * v : 8 * v + 8, :]
            w_ref[8 * v : 8 * v + 8, :] = run * alpha
            run = run * (1.0 - alpha)
        ahead = scan_rows(run, None, 1.0, True, lambda u, w: u * w)
        for v in range(steps):
            w_ref[8 * v : 8 * v + 8, :] *= ahead

        yield
        colours = [z.astype(F32) for z in split(colour, 3)]
        ch, cm, cl = colours
        wh, wl = split(w_ref[...], 2)
        stacked = pad_rows(colours, 16).astype(BF16)
        picture = dot(stacked, wh) + dot(stacked, wl)
        yield
        picture = picture[0:3] + picture[3:6] + picture[6:9]
        lanes = pl.ds(pl.multiple_of(t * PIX, PIX), PIX)
        rendered_ref[:, lanes] = picture
        error = picture - target_ref[:, lanes]
        errors = [z.astype(F32) for z in split(error, 3)]
        eh, em, el = errors
        dw = dot(
            pad_rows([ch, ch, ch, cm, cm, cl], 32).astype(BF16),
            pad_rows([eh, em, el, eh, em, eh], 32).astype(BF16),
            TN,
        )
        stacked = pad_rows(errors, 16).astype(BF16)
        dcol = dot(stacked, wh, NT) + dot(stacked, wl, NT)
        yield
        dcol = dcol[0:3] + dcol[3:6] + dcol[6:9]

        h_ref[...] = dw * w_ref[...]
        run = jnp.zeros((8, PIX), F32)
        for v in range(steps):
            run = run + h_ref[8 * v : 8 * v + 8, :]
        behind = scan_rows(run, None, 0.0, False, lambda u, w: u + w)
        for v in reversed(range(steps)):
            alpha = alpha_ref[8 * v : 8 * v + 8, :]
            u = h_ref[8 * v : 8 * v + 8, :]
            h_ref[8 * v : 8 * v + 8, :] = u - behind * (alpha * inverse(1.0 - alpha))
            behind = behind + u

        yield
        h = h_ref[...]

        def moment(z):
            zh, zl = split(z, 2)
            return dot(moments, zh, NT) + dot(moments, zl, NT)

        m0, m1, m2 = moment(h), moment(-h * f1_ref[...]), moment(-h * f2_ref[...])
        yield
        s1, s2 = m1[0:1], m2[0:1]
        grads = pad_rows(
            [
                -a * s1,
                -b * s1 - c2 * s2,
                m1[1:2] - mx * s1,
                m1[2:3] - my * s1,
                m2[2:3] - my * s2,
                unsig * m0[0:1],
                dcol,
            ],
            PARAMS,
        )
        puts.append(scatter(grads, place, mine))

    group = len(tile_refs)

    def some(i, carry):
        puts = []
        lockstep(tile(i * group + j, tile_refs[j], puts) for j in range(group))
        total_ref[...] += sum(puts[1:], puts[0])
        return carry

    lax.fori_loop(0, tiles // group, some, 0)
    for c in range(PARAMS):
        out_ref[:, c, :] = total_ref[c * cells : (c + 1) * cells, :]


def collect(part, row, groups):
    low = one_hot(row & (LANES - 1), LANES).astype(BF16)
    return scatter(part, low, one_hot(row >> 7, groups))


def splatting(
    splats_ref, depth_ref, owner_ref, row_ref, count_ref, target_ref, rendered_ref, grad_ref,
    order_ref, own_ref, pos_ref, ask_ref, asked_ref, reply_ref, values_ref, out_ref, incoming_ref,
    parts_ref, lookup_ref, sums_ref, shade_refs, send_sem, recv_sem,
):
    cells = ask_ref.shape[0]
    me = lax.axis_index("cell")
    barrier = pltpu.get_barrier_semaphore()

    def greet(step, carry):
        pl.semaphore_signal(
            barrier, inc=1, device_id=(lax.rem(me + step, cells),), device_id_type=pl.DeviceIdType.MESH
        )
        return carry

    def over_others(body):
        def one(step, carry):
            body(lax.rem(me + step, cells), lax.rem(me + cells - step, cells))
            return carry

        lax.fori_loop(1, cells, one, 0)

    def copy(phase, source_ref, landing_ref, to, slot):
        return pltpu.make_async_remote_copy(
            src_ref=source_ref.at[to],
            dst_ref=landing_ref.at[slot],
            send_sem=send_sem.at[phase, to],
            recv_sem=recv_sem.at[phase, slot],
            device_id=(to,),
            device_id_type=pl.DeviceIdType.MESH,
        )

    lax.fori_loop(1, cells, greet, 0)
    plan_slots(depth_ref, order_ref, owner_ref, row_ref, own_ref, pos_ref, ask_ref, parts_ref)
    lookup_ref[...] = splat_table(splats_ref, sums_ref)
    pl.semaphore_wait(barrier, cells - 1)
    over_others(lambda to, source: copy(0, ask_ref, asked_ref, to, me).start())

    def in_groups(body):
        size = group_of(cells, 8)
        body([0] + list(range(1, size)), True)

        def one(i, carry):
            body([i * size + j for j in range(size)], False)
            return carry

        lax.fori_loop(1, cells // size, one, 0)

    def source_at(step):
        return lax.rem(me + cells - step, cells)

    def serve(steps, first):
        sources = [source_at(step) for step in steps]
        if first:
            asked_ref[me] = ask_ref[me]
        for source in sources[1 if first else 0 :]:
            copy(0, ask_ref, asked_ref, source, source).wait_recv()
        replies = [answer(lookup_ref, asked_ref[source]) for source in sources]
        if first:
            values_ref[me] = replies[0]
        for source, reply in list(zip(sources, replies))[1 if first else 0 :]:
            reply_ref[source] = reply
            copy(1, reply_ref, values_ref, source, me).start()

    in_groups(serve)
    over_others(lambda to, source: copy(0, ask_ref, asked_ref, to, me).wait_send())
    over_others(lambda to, source: copy(1, reply_ref, values_ref, source, source).wait_recv())
    shade(
        values_ref, own_ref, pos_ref, order_ref, count_ref, target_ref, rendered_ref, out_ref,
        *shade_refs,
    )
    over_others(lambda to, source: copy(2, out_ref, incoming_ref, to, me).start())
    sums_ref[...] = jnp.zeros_like(sums_ref)
    over_others(lambda to, source: copy(1, reply_ref, values_ref, to, me).wait_send())
    groups = sums_ref.shape[0] // PARAMS

    def receive(steps, first):
        sources = [source_at(step) for step in steps]
        for source in sources[1 if first else 0 :]:
            copy(2, out_ref, incoming_ref, source, source).wait_recv()
        parts = [incoming_ref[source] for source in sources[1 if first else 0 :]]
        if first:
            parts = [out_ref[me]] + parts
        added = [collect(part, asked_ref[source], groups) for part, source in zip(parts, sources)]
        sums_ref[...] += sum(added[1:], added[0])

    in_groups(receive)
    grad_ref[...] = sums_ref[...]

    over_others(lambda to, source: copy(2, out_ref, incoming_ref, to, me).wait_send())


def per_device(splats, target, slot_owner, slot_row, depth_order, tile_count):
    cells = lax.axis_size("cell")
    owned = splats.shape[1]
    tiles, block = slot_row.shape
    cap = max(2, 2 * tiles * block // cells)
    owner = slot_owner.reshape(tiles, block)
    grouped = PARAMS * (owned // LANES)
    vmem = pltpu.VMEM
    rendered, grad = pl.pallas_call(
        splatting,
        out_shape=(
            jax.ShapeDtypeStruct(target.shape, F32),
            jax.ShapeDtypeStruct((grouped, LANES), F32),
        ),
        in_specs=[pl.BlockSpec(memory_space=pltpu.VMEM)] * 6,
        out_specs=[pl.BlockSpec(memory_space=pltpu.VMEM)] * 2,
        scratch_shapes=[
            vmem((tiles, block), I32),
            vmem((tiles, block), I32),
            vmem((tiles, block), I32),
            vmem((cells, 1, cap), I32),
            vmem((cells, 1, cap), I32),
            vmem((cells, PARAMS, cap), F32),
            vmem((cells, PARAMS, cap), F32),
            vmem((cells, PARAMS, cap), F32),
            vmem((cells, PARAMS, cap), F32),
            vmem((2 * cells, cap), F32),
            vmem((grouped, 3 * LANES), BF16),
            vmem((grouped, LANES), F32),
            [
                vmem((PARAMS * cells, cap), F32),
                vmem((PARAMS * cells, 3 * cap), BF16),
                [[vmem((block, PIX), F32)] * 5] * group_of(tiles, 4),
            ],
            pltpu.SemaphoreType.DMA((3, cells)),
            pltpu.SemaphoreType.DMA((3, cells)),
        ],
        compiler_params=pltpu.CompilerParams(
            vmem_limit_bytes=48 * 1024 * 1024, collective_id=0, has_side_effects=True
        ),
    )(splats, depth_order, owner, slot_row, tile_count.reshape(tiles, 1), target)
    return (rendered, grad.reshape(PARAMS, owned))


def solution(mesh):
    in_specs = (
        P(None, "cell"),
        P(None, "cell"),
        P("cell", None, None),
        P("cell", None),
        P("cell", None),
        P("cell"),
    )
    out_specs = (P(None, "cell"), P(None, "cell"))
    return jax.shard_map(
        per_device, mesh=mesh, in_specs=in_specs, out_specs=out_specs, check_vma=False
    )
```

```python
import jax
import jax.numpy as jnp
from jax import lax
from jax.experimental import pallas as pl
from jax.experimental.pallas import tpu as pltpu
from jax.sharding import PartitionSpec as P

SIDE = 16
PIX = SIDE * SIDE
PARAMS = 9
LANES = 128
F32, BF16, I32 = jnp.float32, jnp.bfloat16, jnp.int32
NT = (((1,), (1,)), ((), ()))
TN = (((0,), (0,)), ((), ()))


def split(x, parts):
    out = []
    for part in range(parts):
        out.append(x.astype(BF16))
        if part < parts - 1:
            x = x - out[-1].astype(F32)
    return out


def dot(a, b, dims=(((1,), (0,)), ((), ()))):
    return lax.dot_general(a, b, dims, preferred_element_type=F32)


def iota(shape, axis):
    return lax.broadcasted_iota(I32, shape, axis)


def one_hot(index, count):
    return jnp.where(iota((count, index.shape[1]), 0) == index, 1.0, 0.0)


def inverse(x):
    guess = pl.reciprocal(x, approx=True)
    return guess * (2.0 - x * guess)


def pad_rows(pieces, count):
    have = sum(piece.shape[0] for piece in pieces)
    if have < count:
        pieces = list(pieces) + [jnp.zeros((count - have, pieces[0].shape[1]), F32)]
    return jnp.concatenate(pieces, axis=0)


def lockstep(works):
    works = list(works)
    while works:
        works = [work for work in works if next(work, "end") is None]


def group_of(count, most):
    return next(size for size in range(most, 0, -1) if count % size == 0)


def gather(table, place, mask):
    found = dot(table, jnp.concatenate([place, place, place], axis=0))
    high = mask.shape[0]
    return [
        jnp.sum(found[c * high : (c + 1) * high] * mask, axis=0, keepdims=True) for c in range(PARAMS)
    ]


def scatter(rows, place, mask):
    mask = mask.astype(BF16)
    pieces = split(rows, 2)
    spread = jnp.concatenate(
        [
            jnp.concatenate([piece[c : c + 1] * mask for c in range(PARAMS)], axis=0)
            for piece in pieces
        ],
        axis=1,
    )
    return dot(spread, jnp.concatenate([place, place], axis=1), NT)


def plan_slots(depth_ref, order_ref, owner_ref, row_ref, own_ref, pos_ref, ask_ref, parts_ref):
    tiles, block = order_ref.shape
    cells, _, cap = ask_ref.shape
    slot, place = iota((block, block), 0), iota((block, block), 1)
    strided = jnp.where(slot == (place & 7) * (block // 8) + (place >> 3), 1.0, 0.0).astype(BF16)
    order_ref[...] = dot(depth_ref[...].astype(F32).astype(BF16), strided).astype(I32)
    before = jnp.where(iota((block, block), 0) < iota((block, block), 1), 1.0, 0.0).astype(BF16)
    parts_ref[...] = jnp.zeros_like(parts_ref)
    group = group_of(tiles, 8)

    def tile(t, state, asks):
        at = pl.ds(t, 1)
        chosen = one_hot(order_ref[at, :], block).astype(BF16)
        row = row_ref[at, :]
        source = pad_rows(
            [owner_ref[at, :].astype(F32), (row >> 8).astype(F32), (row & 255).astype(F32)], 16
        )
        moved = dot(source.astype(BF16), chosen)
        yield
        own = moved[0:1].astype(I32)
        own_ref[at, :] = own
        mine = one_hot(own, cells)
        within = dot(mine.astype(BF16), before)
        asked = jnp.concatenate([mine * moved[1:2], mine * moved[2:3]], axis=0).astype(BF16)
        earlier = within + state[0]
        state[0] = state[0] + jnp.sum(mine, axis=1, keepdims=True)
        yield
        pos = jnp.sum(mine * earlier, axis=0, keepdims=True).astype(I32)
        pos_ref[at, :] = pos
        asks.append(dot(asked, one_hot(pos, cap).astype(BF16), NT))

    def some(i, seen):
        state, asks = [seen], []
        lockstep(tile(i * group + j, state, asks) for j in range(group))
        parts_ref[...] += sum(asks[1:], asks[0])
        return state[0]

    lax.fori_loop(0, tiles // group, some, jnp.zeros((cells, 1), F32))
    both = parts_ref[...].astype(I32)
    both = both[:cells] * 256 + both[cells:]
    for c in range(cells):
        ask_ref[c] = both[c : c + 1]


def splat_table(splats_ref, rows_ref):
    groups = splats_ref.shape[1] // LANES
    for c in range(PARAMS):
        for g in range(groups):
            at = c * groups + g
            rows_ref[at : at + 1, :] = splats_ref[c : c + 1, g * LANES : (g + 1) * LANES]
    return jnp.concatenate(split(rows_ref[...], 3), axis=1)


def answer(lookup_ref, row):
    low = one_hot(row & (LANES - 1), LANES).astype(BF16)
    mask = one_hot(row >> 7, lookup_ref.shape[0] // PARAMS)
    return jnp.concatenate(gather(lookup_ref[...], low, mask), axis=0)


def scan_rows(x, keep, fill, down, combine):
    at = iota(x.shape, 0)

    def moved(y, by):
        if down:
            return jnp.where(at >= by, pltpu.roll(y, by, 0), fill)
        return jnp.where(at < 8 - by, pltpu.roll(y, 8 - by, 0), fill)

    x = moved(x, 1)
    for by in (1, 2, 4):
        x = combine(x, moved(x, by))
    return x


def shade(
    values_ref, own_ref, pos_ref, order_ref, count_ref, target_ref, rendered_ref, out_ref,
    total_ref, table_ref, tile_refs,
):
    tiles, block = own_ref.shape
    cells, _, cap = values_ref.shape
    steps = block // 8
    pixel = iota((1, PIX), 1)
    x = (pixel % SIDE).astype(F32) + (0.5 - SIDE / 2)
    y = (pixel // SIDE).astype(F32) + (0.5 - SIDE / 2)
    one, zero = jnp.ones((1, PIX), F32), jnp.zeros((1, PIX), F32)
    linear = jnp.concatenate(
        [
            pad_rows([x, y, one], 8),
            pad_rows([zero, zero, zero, y, one], 8),
            pad_rows([zero, zero, zero, zero, zero, one], 8),
        ],
        axis=1,
    )
    linear = pad_rows([linear, linear, linear], 32).astype(BF16)
    moments = pad_rows([one, x, y], 16).astype(BF16)

    for c in range(PARAMS):
        for part, piece in enumerate(split(values_ref[:, c, :], 3)):
            table_ref[c * cells : (c + 1) * cells, part * cap : (part + 1) * cap] = piece
    total_ref[...] = jnp.zeros_like(total_ref)

    def tile(t, refs, puts):
        f1_ref, f2_ref, alpha_ref, w_ref, h_ref = refs
        at = pl.ds(t, 1)
        own = own_ref[at, :]
        place = one_hot(pos_ref[at, :], cap).astype(BF16)
        mine = one_hot(own, cells)
        p = gather(table_ref[...], place, mine)
        yield
        live = jnp.where(order_ref[at, :] < count_ref[at, :], 1.0, 0.0)
        mx, my = p[0] - SIDE / 2, p[1] - SIDE / 2
        a, b, c2 = p[2], p[3], p[4]
        colour = jnp.concatenate(p[6:9], axis=0)
        sig = 1.0 / (1.0 + jnp.exp(-p[5]))
        unsig = 1.0 / (1.0 + jnp.exp(p[5]))
        factors = pad_rows([a, b, -(a * mx + b * my), c2, -(c2 * my), sig * live], 8)
        factors = pad_rows([z.astype(F32) for z in split(factors, 3)], 32).astype(BF16)
        spread = dot(factors, linear, TN)
        yield
        f1, f2 = spread[:, :PIX], spread[:, PIX : 2 * PIX]
        f1_ref[...] = f1
        f2_ref[...] = f2
        alpha_ref[...] = spread[:, 2 * PIX :] * jnp.exp(-0.5 * (f1 * f1 + f2 * f2))

        yield
        run = jnp.ones((8, PIX), F32)
        for v in range(steps):
            alpha = alpha_ref[8 * v : 8 * v + 8, :]
            w_ref[8 * v : 8 * v + 8, :] = run * alpha
            run = run * (1.0 - alpha)
        ahead = scan_rows(run, None, 1.0, True, lambda u, w: u * w)
        for v in range(steps):
            w_ref[8 * v : 8 * v + 8, :] *= ahead

        yield
        colours = [z.astype(F32) for z in split(colour, 3)]
        ch, cm, cl = colours
        wh, wl = split(w_ref[...], 2)
        stacked = pad_rows(colours, 16).astype(BF16)
        picture = dot(stacked, wh) + dot(stacked, wl)
        yield
        picture = picture[0:3] + picture[3:6] + picture[6:9]
        lanes = pl.ds(pl.multiple_of(t * PIX, PIX), PIX)
        rendered_ref[:, lanes] = picture
        error = picture - target_ref[:, lanes]
        errors = [z.astype(F32) for z in split(error, 3)]
        eh, em, el = errors
        dw = dot(
            pad_rows([ch, ch, ch, cm, cm, cl], 32).astype(BF16),
            pad_rows([eh, em, el, eh, em, eh], 32).astype(BF16),
            TN,
        )
        stacked = pad_rows(errors, 16).astype(BF16)
        dcol = dot(stacked, wh, NT) + dot(stacked, wl, NT)
        yield
        dcol = dcol[0:3] + dcol[3:6] + dcol[6:9]

        h_ref[...] = dw * w_ref[...]
        run = jnp.zeros((8, PIX), F32)
        for v in range(steps):
            run = run + h_ref[8 * v : 8 * v + 8, :]
        behind = scan_rows(run, None, 0.0, False, lambda u, w: u + w)
        for v in reversed(range(steps)):
            alpha = alpha_ref[8 * v : 8 * v + 8, :]
            u = h_ref[8 * v : 8 * v + 8, :]
            h_ref[8 * v : 8 * v + 8, :] = u - behind * (alpha * inverse(1.0 - alpha))
            behind = behind + u

        yield
        h = h_ref[...]

        def moment(z):
            zh, zl = split(z, 2)
            return dot(moments, zh, NT) + dot(moments, zl, NT)

        m0, m1, m2 = moment(h), moment(-h * f1_ref[...]), moment(-h * f2_ref[...])
        yield
        s1, s2 = m1[0:1], m2[0:1]
        grads = pad_rows(
            [
                -a * s1,
                -b * s1 - c2 * s2,
                m1[1:2] - mx * s1,
                m1[2:3] - my * s1,
                m2[2:3] - my * s2,
                unsig * m0[0:1],
                dcol,
            ],
            PARAMS,
        )
        puts.append(scatter(grads, place, mine))

    group = len(tile_refs)

    def some(i, carry):
        puts = []
        lockstep(tile(i * group + j, tile_refs[j], puts) for j in range(group))
        total_ref[...] += sum(puts[1:], puts[0])
        return carry

    lax.fori_loop(0, tiles // group, some, 0)
    for c in range(PARAMS):
        out_ref[:, c, :] = total_ref[c * cells : (c + 1) * cells, :]


def collect(part, row, groups):
    low = one_hot(row & (LANES - 1), LANES).astype(BF16)
    return scatter(part, low, one_hot(row >> 7, groups))


def splatting(
    splats_ref, depth_ref, owner_ref, row_ref, count_ref, target_ref, rendered_ref, grad_ref,
    order_ref, own_ref, pos_ref, ask_ref, asked_ref, reply_ref, values_ref, out_ref, incoming_ref,
    parts_ref, lookup_ref, sums_ref, shade_refs, send_sem, recv_sem,
):
    cells = ask_ref.shape[0]
    me = lax.axis_index("cell")
    barrier = pltpu.get_barrier_semaphore()

    def greet(step, carry):
        pl.semaphore_signal(
            barrier, inc=1, device_id=(lax.rem(me + step, cells),), device_id_type=pl.DeviceIdType.MESH
        )
        return carry

    def over_others(body):
        def one(step, carry):
            body(lax.rem(me + step, cells), lax.rem(me + cells - step, cells))
            return carry

        lax.fori_loop(1, cells, one, 0)

    def copy(phase, source_ref, landing_ref, to, slot):
        return pltpu.make_async_remote_copy(
            src_ref=source_ref.at[to],
            dst_ref=landing_ref.at[slot],
            send_sem=send_sem.at[phase, to],
            recv_sem=recv_sem.at[phase, slot],
            device_id=(to,),
            device_id_type=pl.DeviceIdType.MESH,
        )

    lax.fori_loop(1, cells, greet, 0)
    plan_slots(depth_ref, order_ref, owner_ref, row_ref, own_ref, pos_ref, ask_ref, parts_ref)
    lookup_ref[...] = splat_table(splats_ref, sums_ref)
    pl.semaphore_wait(barrier, cells - 1)
    over_others(lambda to, source: copy(0, ask_ref, asked_ref, to, me).start())

    def in_groups(body):
        size = group_of(cells, 8)
        body([0] + list(range(1, size)), True)

        def one(i, carry):
            body([i * size + j for j in range(size)], False)
            return carry

        lax.fori_loop(1, cells // size, one, 0)

    def source_at(step):
        return lax.rem(me + cells - step, cells)

    def serve(steps, first):
        sources = [source_at(step) for step in steps]
        if first:
            asked_ref[me] = ask_ref[me]
        for source in sources[1 if first else 0 :]:
            copy(0, ask_ref, asked_ref, source, source).wait_recv()
        replies = [answer(lookup_ref, asked_ref[source]) for source in sources]
        if first:
            values_ref[me] = replies[0]
        for source, reply in list(zip(sources, replies))[1 if first else 0 :]:
            reply_ref[source] = reply
            copy(1, reply_ref, values_ref, source, me).start()

    in_groups(serve)
    over_others(lambda to, source: copy(0, ask_ref, asked_ref, to, me).wait_send())
    over_others(lambda to, source: copy(1, reply_ref, values_ref, source, source).wait_recv())
    shade(
        values_ref, own_ref, pos_ref, order_ref, count_ref, target_ref, rendered_ref, out_ref,
        *shade_refs,
    )
    over_others(lambda to, source: copy(2, out_ref, incoming_ref, to, me).start())
    sums_ref[...] = jnp.zeros_like(sums_ref)
    over_others(lambda to, source: copy(1, reply_ref, values_ref, to, me).wait_send())
    groups = sums_ref.shape[0] // PARAMS

    def receive(steps, first):
        sources = [source_at(step) for step in steps]
        for source in sources[1 if first else 0 :]:
            copy(2, out_ref, incoming_ref, source, source).wait_recv()
        parts = [incoming_ref[source] for source in sources[1 if first else 0 :]]
        if first:
            parts = [out_ref[me]] + parts
        added = [collect(part, asked_ref[source], groups) for part, source in zip(parts, sources)]
        sums_ref[...] += sum(added[1:], added[0])

    in_groups(receive)
    grad_ref[...] = sums_ref[...]

    over_others(lambda to, source: copy(2, out_ref, incoming_ref, to, me).wait_send())


def per_device(splats, target, slot_owner, slot_row, depth_order, tile_count):
    cells = lax.axis_size("cell")
    owned = splats.shape[1]
    tiles, block = slot_row.shape
    cap = max(2, 2 * tiles * block // cells)
    owner = slot_owner.reshape(tiles, block)
    grouped = PARAMS * (owned // LANES)
    vmem = pltpu.VMEM
    rendered, grad = pl.pallas_call(
        splatting,
        out_shape=(
            jax.ShapeDtypeStruct(target.shape, F32),
            jax.ShapeDtypeStruct((grouped, LANES), F32),
        ),
        in_specs=[pl.BlockSpec(memory_space=pltpu.VMEM)] * 6,
        out_specs=[pl.BlockSpec(memory_space=pltpu.VMEM)] * 2,
        scratch_shapes=[
            vmem((tiles, block), I32),
            vmem((tiles, block), I32),
            vmem((tiles, block), I32),
            vmem((cells, 1, cap), I32),
            vmem((cells, 1, cap), I32),
            vmem((cells, PARAMS, cap), F32),
            vmem((cells, PARAMS, cap), F32),
            vmem((cells, PARAMS, cap), F32),
            vmem((cells, PARAMS, cap), F32),
            vmem((2 * cells, cap), F32),
            vmem((grouped, 3 * LANES), BF16),
            vmem((grouped, LANES), F32),
            [
                vmem((PARAMS * cells, cap), F32),
                vmem((PARAMS * cells, 3 * cap), BF16),
                [[vmem((block, PIX), F32)] * 5] * group_of(tiles, 8),
            ],
            pltpu.SemaphoreType.DMA((3, cells)),
            pltpu.SemaphoreType.DMA((3, cells)),
        ],
        compiler_params=pltpu.CompilerParams(
            vmem_limit_bytes=48 * 1024 * 1024, collective_id=0, has_side_effects=True
        ),
    )(splats, depth_order, owner, slot_row, tile_count.reshape(tiles, 1), target)
    return (rendered, grad.reshape(PARAMS, owned))


def solution(mesh):
    in_specs = (
        P(None, "cell"),
        P(None, "cell"),
        P("cell", None, None),
        P("cell", None),
        P("cell", None),
        P("cell"),
    )
    out_specs = (P(None, "cell"), P(None, "cell"))
    return jax.shard_map(
        per_device, mesh=mesh, in_specs=in_specs, out_specs=out_specs, check_vma=False
    )
```
